32 devices in a mesh: dp: 4 (over z), tensor: 4 (over x, core), context: 2 (over y).
Axes of the slice: x: 2, y: 2, z: 4, core: 2. Of those that a mesh axis runs over, the one named last changes fastest.
Arguments:
- inputs: bfloat16 [4, 4096, 256], P('dp', 'tensor', 'context'), may hold values from -6 to 6
- out_grad: bfloat16 [4, 4096, 256], P('dp', 'tensor', 'context'), may hold values from -6 to 6
- filters: float32 [256, 256], P('tensor', 'context'), may hold values from -0.375 to 0.375
- skip: float32 [4096], P('tensor'), may hold values from 0.5 to 1.5
Outputs:
- grad_input: bfloat16 [4, 4096, 256], P('dp', 'tensor', 'context')
- grad_filter: float32 [256, 256], P('tensor', 'context')
The draws below stay inside these ranges and needn't reach their ends.
All inputs are finite; a program needn't handle non-finite values.
Results may differ from the reference program's by a relative error of at most 0.0034.
Values may be sent and summed in bfloat16 or wider, within the bound.
No kernel may reach another device: no remote copies, remote signals or barrier semaphores. Data moves between devices by JAX's collectives and lax.ppermute only.
A program may use at most 64 MiB of HBM per device.

```python
import math
import jax
import jax.numpy as jnp

GROUP = 16
GROUPS = 256
CHANNELS = 4096
SEQ = 256
BATCH = 4


def levels(own_key, dims, shards, low, high):
    def one(position, parts):
        heights = jax.random.uniform(jax.random.fold_in(jax.random.fold_in(own_key, 6), position), (parts,), jnp.float32, low / len(shards), high / len(shards))
        return jnp.repeat(jnp.exp(heights), dims[position] // parts).reshape((-1,) + (1,) * (len(dims) - position - 1))

    level = one(*shards[0])
    for cut in shards[1:]:
        level = level * one(*cut)
    return level


def bell_draw(stream_key, extent, spread, most, shards=(), dtype=jnp.bfloat16):
    factor_of = levels(stream_key, extent, shards, -0.22, 0.18) if shards else 1.0
    drawn = jax.random.normal(stream_key, extent, jnp.float32) * spread * factor_of
    return jnp.minimum(jnp.maximum(drawn, -most), most).astype(dtype)


def setup_inputs(seed: int = 0) -> dict:
    arg_keys = jax.random.split(jax.random.key(seed), 5)
    inputs = bell_draw(arg_keys[0], (BATCH, CHANNELS, SEQ), 1.0, 6.0, ((0, 4), (1, 4), (2, 2)))
    out_grad = bell_draw(arg_keys[1], (BATCH, CHANNELS, SEQ), 1.0, 6.0, ((0, 4), (1, 4), (2, 2)))
    filters = bell_draw(arg_keys[2], (GROUPS, SEQ), SEQ ** -0.5, 0.375, ((0, 4), (1, 2)), jnp.float32)
    skip = jnp.clip(0.5 + 1.0 * jax.random.uniform(arg_keys[3], (CHANNELS,), jnp.float32) ** levels(arg_keys[3], (CHANNELS,), ((0, 4),), -0.2, 0.2), 0.5, 1.5)
    return dict(inputs=inputs, out_grad=out_grad, filters=filters, skip=skip)


def reference(inputs, out_grad, filters, skip):
    padded_len = 2 * SEQ
    filter_spec = jnp.fft.rfft(filters, n=padded_len, axis=-1)
    channel_spec = jnp.repeat(filter_spec, GROUP, axis=0)
    gradients = []
    filter_sum = jnp.zeros((GROUPS, SEQ), jnp.float32)
    for sequence in range(BATCH):
        signal = inputs[sequence].astype(jnp.float32)
        upstream = out_grad[sequence].astype(jnp.float32)
        sig_spec = jnp.fft.rfft(signal, n=padded_len, axis=-1)
        up_spec = jnp.fft.rfft(upstream, n=padded_len, axis=-1)
        correlated = jnp.fft.irfft(jnp.conj(channel_spec) * up_spec, n=padded_len, axis=-1)[:, :SEQ]
        correlated = correlated.astype(jnp.float32).astype(jnp.bfloat16)
        gradients.append((correlated.astype(jnp.float32) + skip[:, None] * upstream).astype(jnp.bfloat16))
        lagged = jnp.fft.irfft(jnp.conj(sig_spec) * up_spec, n=padded_len, axis=-1)[:, :SEQ]
        filter_sum = filter_sum + lagged.reshape(GROUPS, GROUP, SEQ).sum(axis=1).astype(jnp.float32)
    norm_scale = 1.0 / math.sqrt(BATCH * GROUP * SEQ)
    return (jnp.stack(gradients), filter_sum * norm_scale)
```

```python
import math

import jax
import jax.numpy as jnp
import numpy as np
from jax import lax
from jax.experimental import pallas as pl
from jax.experimental.pallas import tpu as pltpu
from jax.sharding import PartitionSpec as P

GROUP = 16


exact_mode = lax.Precision.HIGHEST


def block_tables(tok):
    step = np.arange(tok)
    angle = np.pi / tok * np.outer(step, step + 0.5)
    forward = np.concatenate([np.cos(angle), -np.sin(angle)], axis=1)
    inverse = np.concatenate([np.cos(angle).T, -np.sin(angle).T], axis=0) / tok
    pair = []
    for table, axis in ((forward, 0), (inverse, 1)):
        high = table.astype(jnp.bfloat16)
        low = (table - high.astype(np.float64)).astype(jnp.bfloat16)
        pair.append(jnp.asarray(np.concatenate([high, low], axis=axis)))
    return pair


def matmul(left, right):
    return jnp.dot(left, right, preferred_element_type=jnp.float32)


def split(value):
    high = value.astype(jnp.bfloat16)
    return high, (value - high.astype(jnp.float32)).astype(jnp.bfloat16)


def forward_exact(block, forward):
    return matmul(jnp.concatenate([block, block], axis=1), forward)


def forward_float(value, forward):
    high, low = split(value)
    return forward_exact(high, forward) + matmul(low, forward[: value.shape[1]])


def inverse_float(spec, inverse):
    tok = spec.shape[1] // 2
    high, low = split(spec)
    both = matmul(high, inverse)
    return both[:, :tok] + both[:, tok:] + matmul(low, inverse[:, :tok])


def conj_mul(left, right):
    tok = left.shape[1] // 2
    left_re, left_im = left[:, :tok], left[:, tok:]
    right_re, right_im = right[:, :tok], right[:, tok:]
    return (
        left_re * right_re + left_im * right_im,
        left_re * right_im - left_im * right_re,
    )


def group_sum(value):
    rows, width = value.shape
    return value.reshape(rows // GROUP, GROUP, width).sum(axis=1)


def group_spread(value):
    rows, width = value.shape
    return jnp.broadcast_to(value[:, None, :], (rows, GROUP, width)).reshape(rows * GROUP, width)


def sign_row(tok):
    lane = lax.broadcasted_iota(jnp.int32, (1, tok), 1)
    return (1 - 2 * (lane % 2)).astype(jnp.float32)


def local_lag_kernel(in_ref, grad_ref, forward_ref, inverse_ref, part_ref, lag_ref, taps_ref):
    first = lax.axis_index("context") == 0
    chans, tok = in_ref.shape
    rows = GROUP * 8
    forward = forward_ref[...]
    for start in range(0, chans, rows):
        span = pl.ds(start, rows)
        groups = pl.ds(start // GROUP, rows // GROUP)
        in_spec = forward_exact(in_ref[span, :], forward)
        grad_spec = forward_exact(grad_ref[span, :], forward)
        lag_re, lag_im = conj_mul(in_spec, grad_spec)
        lag_ref[groups, :tok] = group_sum(lag_re)
        lag_ref[groups, tok:] = group_sum(lag_im)
        part_ref[span, :] = jnp.where(first, in_spec, grad_spec)
    taps_ref[...] = inverse_float(lag_ref[...], inverse_ref[...])


def cross_lag_kernel(moved_ref, part_ref, lag_ref, taps_ref, forward_ref, inverse_ref, out_ref, sum_ref):
    first = lax.axis_index("context") == 0
    chans, tok = moved_ref.shape
    rows = GROUP * 8
    forward = forward_ref[...]
    for start in range(0, chans, rows):
        span = pl.ds(start, rows)
        groups = pl.ds(start // GROUP, rows // GROUP)
        spec = forward_exact(moved_ref[span, :], forward)
        re, im = conj_mul(part_ref[span, :], spec)
        sum_ref[groups, :tok] = group_sum(re)
        sum_ref[groups, tok:] = group_sum(im)
    sign = sign_row(tok)
    re, im = sum_ref[:, :tok], sum_ref[:, tok:]
    total = jnp.concatenate(
        [
            jnp.where(first, lag_ref[:, :tok] + sign * im, re),
            jnp.where(first, lag_ref[:, tok:] - sign * re, -im),
        ],
        axis=1,
    )
    taps = inverse_float(total, inverse_ref[...])
    out_ref[...] = taps + jnp.where(first, taps_ref[...], 0.0)


def local_corr_kernel(grad_ref, own_ref, other_ref, forward_ref, inverse_ref, corr_ref, turn_ref, base_ref):
    first = lax.axis_index("context") == 0
    chans, tok = grad_ref.shape
    rows = GROUP * 8
    forward = forward_ref[...]
    inverse = inverse_ref[...]
    base = forward_float(jnp.where(first, own_ref[...], other_ref[...]), forward)
    tail = forward_float(jnp.where(first, other_ref[...], own_ref[...]), forward)
    base_ref[...] = base
    sign = sign_row(tok)
    turn_ref[:, :tok] = jnp.where(first, tail[:, :tok] - sign * base[:, tok:], 0.0)
    turn_ref[:, tok:] = jnp.where(first, tail[:, tok:] + sign * base[:, :tok], 0.0)
    for start in range(0, chans, rows):
        span = pl.ds(start, rows)
        groups = pl.ds(start // GROUP, rows // GROUP)
        spec = forward_exact(grad_ref[span, :], forward)
        prod = conj_mul(group_spread(base_ref[groups, :]), spec)
        corr_ref[span, :] = inverse_float(jnp.concatenate(prod, axis=1), inverse)


def cross_corr_kernel(moved_ref, grad_ref, skip_ref, corr_ref, turn_ref, forward_ref, inverse_ref, out_ref):
    chans, tok = moved_ref.shape
    rows = GROUP * 8
    forward = forward_ref[...]
    inverse = inverse_ref[...]
    for start in range(0, chans, rows):
        span = pl.ds(start, rows)
        groups = pl.ds(start // GROUP, rows // GROUP)
        spec = forward_exact(moved_ref[span, :], forward)
        prod = conj_mul(group_spread(turn_ref[groups, :]), spec)
        corr = corr_ref[span, :] + inverse_float(jnp.concatenate(prod, axis=1), inverse)
        corr = corr.astype(jnp.bfloat16).astype(jnp.float32)
        gain = jnp.broadcast_to(skip_ref[start // rows, :][None, :], (tok, rows)).T
        out_ref[span, :] = (corr + gain * grad_ref[span, :].astype(jnp.float32)).astype(jnp.bfloat16)


VMEM_SPEC = pl.BlockSpec(memory_space=pltpu.VMEM)


def call(kernel, out_shape, scratch, cost, *operands):
    return pl.pallas_call(
        kernel,
        out_shape=out_shape,
        in_specs=[VMEM_SPEC] * len(operands),
        out_specs=jax.tree.map(lambda _: VMEM_SPEC, out_shape),
        scratch_shapes=scratch,
        cost_estimate=pl.CostEstimate(flops=cost, bytes_accessed=cost // 256, transcendentals=0),
        compiler_params=pltpu.CompilerParams(vmem_limit_bytes=24 * 1024 * 1024),
    )(*operands)


def in_vmem(value):
    return pltpu.with_memory_space_constraint(value, pltpu.VMEM)


def paired(inputs, out_grad, filters, skip):
    chans, tok = inputs.shape[1:]
    groups = filters.shape[0]
    sequences = lax.axis_size("dp")
    first = lax.axis_index("context") == 0
    swap = [(0, 1), (1, 0)]
    forward, inverse = block_tables(tok)
    own_in, own_grad = inputs[0], out_grad[0]
    skip_rows = skip.reshape(-1, GROUP * 8)
    cost = 4 * chans * tok * tok

    other_filters = lax.ppermute(filters, "context", swap)
    moved = lax.ppermute(jnp.where(first, own_in, own_grad), "context", swap)
    part, lag, taps = call(
        local_lag_kernel,
        (
            pltpu.VMEM((chans, 2 * tok), jnp.float32),
            pltpu.VMEM((groups, 2 * tok), jnp.float32),
            pltpu.VMEM((groups, tok), jnp.float32),
        ),
        [],
        8 * cost,
        own_in, own_grad, forward, inverse,
    )
    other_taps = lax.ppermute(taps, "context", swap)
    corr, turn = call(
        local_corr_kernel,
        (
            pltpu.VMEM((chans, tok), jnp.float32),
            pltpu.VMEM((groups, 2 * tok), jnp.float32),
        ),
        [pltpu.VMEM((groups, 2 * tok), jnp.float32)],
        8 * cost,
        own_grad, filters, other_filters, forward, inverse,
    )
    total = call(
        cross_lag_kernel,
        pltpu.VMEM((groups, tok), jnp.float32),
        [pltpu.VMEM((groups, 2 * tok), jnp.float32)],
        8 * cost,
        in_vmem(moved), part, lag, other_taps, forward, inverse,
    )
    grad_input = call(
        cross_corr_kernel,
        jax.ShapeDtypeStruct((chans, tok), jnp.bfloat16),
        [],
        8 * cost,
        in_vmem(moved), own_grad, skip_rows, corr, turn, forward, inverse,
    )
    step = 1
    while step < sequences:
        total = total + lax.ppermute(total, "dp", [(i, i ^ step) for i in range(sequences)])
        step *= 2
    norm_scale = 1.0 / math.sqrt(sequences * GROUP * 2 * tok)
    return (grad_input[None], total * norm_scale)


def dft_tables(size_one, size_two):
    padded_len = size_one * size_two
    range_one = jnp.arange(size_one, dtype=jnp.int32)
    range_two = jnp.arange(size_two, dtype=jnp.int32)
    angle_one = (range_one[:, None] * range_one[None, :] % size_one).astype(jnp.float32) * (
        -2.0 * math.pi / size_one
    )
    angle_two = (range_two[:, None] * range_two[None, :] % size_two).astype(jnp.float32) * (
        -2.0 * math.pi / size_two
    )
    angle_turn = (range_one[:, None] * range_two[None, :] % padded_len).astype(jnp.float32) * (
        -2.0 * math.pi / padded_len
    )
    return (
        jnp.cos(angle_one),
        jnp.sin(angle_one),
        jnp.cos(angle_two),
        jnp.sin(angle_two),
        jnp.cos(angle_turn),
        jnp.sin(angle_turn),
    )


def left_mul(matrix, operand):
    return jnp.einsum("kj,mjl->mkl", matrix, operand, precision=exact_mode)


def right_mul(operand, matrix):
    return jnp.einsum("mkj,jl->mkl", operand, matrix, precision=exact_mode)


def forward_real(signal, tables):
    one_re, one_im, two_re, two_im, turn_re, turn_im = tables
    half_rows = signal.shape[1]
    step_re = left_mul(one_re[:, :half_rows], signal)
    step_im = left_mul(one_im[:, :half_rows], signal)
    mid_re = step_re * turn_re - step_im * turn_im
    mid_im = step_re * turn_im + step_im * turn_re
    spec_re = right_mul(mid_re, two_re) - right_mul(mid_im, two_im)
    spec_im = right_mul(mid_re, two_im) + right_mul(mid_im, two_re)
    return (spec_re, spec_im)


def inverse_real(spec_re, spec_im, tables, half_rows):
    one_re, one_im, two_re, two_im, turn_re, turn_im = tables
    back_re = right_mul(spec_re, two_re) + right_mul(spec_im, two_im)
    back_im = right_mul(spec_im, two_re) - right_mul(spec_re, two_im)
    mid_re = back_re * turn_re + back_im * turn_im
    mid_im = back_im * turn_re - back_re * turn_im
    padded_len = one_re.shape[0] * two_re.shape[0]
    return (
        left_mul(one_re[:half_rows], mid_re) + left_mul(one_im[:half_rows], mid_im)
    ) / padded_len


def owner_groups(owners, own_ch, own_grp):
    starts = jnp.arange(owners, dtype=jnp.int32)[:, None] * own_ch // GROUP
    return starts + jnp.arange(own_grp, dtype=jnp.int32)[None, :]


def owned(inputs, out_grad, filters, skip):
    tok_dev = inputs.shape[2]
    ch_dev = inputs.shape[1]
    grp_dev = filters.shape[0]
    owners = lax.axis_size("context")
    seq_len = tok_dev * owners
    padded_len = 2 * seq_len
    own_ch = ch_dev // owners
    own_grp = max(1, own_ch // GROUP)
    per_group = own_ch // own_grp
    size_one = 1 << (padded_len.bit_length() - 1) // 2
    while padded_len % size_one != 0:
        size_one = size_one // 2
    size_two = padded_len // size_one
    half_rows = size_one // 2
    tables = dft_tables(size_one, size_two)
    moved_in, moved_grad = (
        lax.all_to_all(inputs, "context", split_axis=1, concat_axis=2, tiled=True),
        lax.all_to_all(out_grad, "context", split_axis=1, concat_axis=2, tiled=True),
    )
    slot_groups = owner_groups(owners, own_ch, own_grp)
    pick_rows = (
        slot_groups[:, :, None] == jnp.arange(grp_dev, dtype=jnp.int32)[None, None, :]
    ).astype(jnp.float32)
    outgoing = jnp.einsum("ojg,gt->ojt", pick_rows, filters, precision=exact_mode)
    own_filter = lax.all_to_all(
        outgoing, "context", split_axis=0, concat_axis=2, tiled=True
    ).reshape(own_grp, seq_len)
    sig_in = moved_in[0].astype(jnp.float32).reshape(own_ch, half_rows, size_two)
    sig_grad = moved_grad[0].astype(jnp.float32).reshape(own_ch, half_rows, size_two)
    in_re, in_im = forward_real(sig_in, tables)
    grad_re, grad_im = forward_real(sig_grad, tables)
    filt_re, filt_im = forward_real(own_filter.reshape(own_grp, half_rows, size_two), tables)
    grad_re4 = grad_re.reshape(own_grp, per_group, size_one, size_two)
    grad_im4 = grad_im.reshape(own_grp, per_group, size_one, size_two)
    filt_re4 = filt_re[:, None]
    filt_im4 = filt_im[:, None]
    prod_re = (filt_re4 * grad_re4 + filt_im4 * grad_im4).reshape(own_ch, size_one, size_two)
    prod_im = (filt_re4 * grad_im4 - filt_im4 * grad_re4).reshape(own_ch, size_one, size_two)
    correlated = (
        inverse_real(prod_re, prod_im, tables, half_rows)
        .reshape(1, own_ch, seq_len)
        .astype(jnp.bfloat16)
    )
    returned = lax.all_to_all(correlated, "context", split_axis=2, concat_axis=1, tiled=True)
    grad_input = (
        returned.astype(jnp.float32) + skip[None, :, None] * out_grad.astype(jnp.float32)
    ).astype(jnp.bfloat16)
    in_re4 = in_re.reshape(own_grp, per_group, size_one, size_two)
    in_im4 = in_im.reshape(own_grp, per_group, size_one, size_two)
    lag_re = (in_re4 * grad_re4 + in_im4 * grad_im4).sum(axis=1)
    lag_im = (in_re4 * grad_im4 - in_im4 * grad_re4).sum(axis=1)
    own_terms = inverse_real(lag_re, lag_im, tables, half_rows).reshape(own_grp, seq_len)
    pieces = lax.all_to_all(
        own_terms.reshape(own_grp, owners, tok_dev),
        "context",
        split_axis=1,
        concat_axis=0,
        tiled=True,
    )
    row_groups = owner_groups(owners, own_ch, own_grp).reshape(-1)
    pick_sum = (jnp.arange(grp_dev, dtype=jnp.int32)[:, None] == row_groups[None, :]).astype(
        jnp.float32
    )
    local_sum = jnp.dot(pick_sum, pieces.reshape(owners * own_grp, tok_dev), precision=exact_mode)
    summed = lax.psum(local_sum, "dp")
    norm_scale = 1.0 / math.sqrt(lax.axis_size("dp") * GROUP * seq_len)
    return (grad_input, summed * norm_scale)


def per_device(inputs, out_grad, filters, skip):
    sequences = lax.axis_size("dp")
    halves = lax.axis_size("context") == 2 and inputs.shape[0] == 1
    if halves and sequences & (sequences - 1) == 0 and inputs.shape[1] % (GROUP * 8) == 0:
        return paired(inputs, out_grad, filters, skip)
    return owned(inputs, out_grad, filters, skip)


def solution(mesh):
    in_specs = (
        P("dp", "tensor", "context"),
        P("dp", "tensor", "context"),
        P("tensor", "context"),
        P("tensor"),
    )
    out_specs = (P("dp", "tensor", "context"), P("tensor", "context"))
    return jax.shard_map(
        per_device, mesh=mesh, in_specs=in_specs, out_specs=out_specs, check_vma=False
    )
```

```python
import math

import jax
import jax.numpy as jnp
import numpy as np
from jax import lax
from jax.experimental import pallas as pl
from jax.experimental.pallas import tpu as pltpu
from jax.sharding import PartitionSpec as P

GROUP = 16


exact_mode = lax.Precision.HIGHEST


def block_tables(tok):
    step = np.arange(tok)
    angle = np.pi / tok * np.outer(step, step + 0.5)
    forward = np.concatenate([np.cos(angle), -np.sin(angle)], axis=1)
    inverse = np.concatenate([np.cos(angle).T, -np.sin(angle).T], axis=0) / tok
    pair = []
    for table, axis in ((forward, 0), (inverse, 1)):
        high = table.astype(jnp.bfloat16)
        low = (table - high.astype(np.float64)).astype(jnp.bfloat16)
        pair.append(jnp.asarray(np.concatenate([high, low], axis=axis)))
    return pair


def matmul(left, right):
    return jnp.dot(left, right, preferred_element_type=jnp.float32)


def split(value):
    high = value.astype(jnp.bfloat16)
    return high, (value - high.astype(jnp.float32)).astype(jnp.bfloat16)


def forward_exact(block, forward):
    return matmul(jnp.concatenate([block, block], axis=1), forward)


def forward_float(value, forward):
    high, low = split(value)
    return forward_exact(high, forward) + matmul(low, forward[: value.shape[1]])


def inverse_float(spec, inverse):
    tok = spec.shape[1] // 2
    high, low = split(spec)
    both = matmul(high, inverse)
    return both[:, :tok] + both[:, tok:] + matmul(low, inverse[:, :tok])


def conj_mul(left, right):
    tok = left.shape[1] // 2
    left_re, left_im = left[:, :tok], left[:, tok:]
    right_re, right_im = right[:, :tok], right[:, tok:]
    return (
        left_re * right_re + left_im * right_im,
        left_re * right_im - left_im * right_re,
    )


def group_sum(value):
    rows, width = value.shape
    return value.reshape(rows // GROUP, GROUP, width).sum(axis=1)


def group_spread(value):
    rows, width = value.shape
    return jnp.broadcast_to(value[:, None, :], (rows, GROUP, width)).reshape(rows * GROUP, width)


def sign_row(tok):
    lane = lax.broadcasted_iota(jnp.int32, (1, tok), 1)
    return (1 - 2 * (lane % 2)).astype(jnp.float32)


def local_lag(in_ref, grad_ref, forward_ref, inverse_ref, part_ref, lag_ref, taps_ref):
    first = lax.axis_index("context") == 0
    chans, tok = in_ref.shape
    rows = GROUP * 8
    forward = forward_ref[...]
    for start in range(0, chans, rows):
        span = pl.ds(start, rows)
        groups = pl.ds(start // GROUP, rows // GROUP)
        in_spec = forward_exact(in_ref[span, :], forward)
        grad_spec = forward_exact(grad_ref[span, :], forward)
        lag_re, lag_im = conj_mul(in_spec, grad_spec)
        lag_ref[groups, :tok] = group_sum(lag_re)
        lag_ref[groups, tok:] = group_sum(lag_im)
        part_ref[span, :] = jnp.where(first, in_spec, grad_spec)
    taps_ref[...] = jnp.where(first, 0.0, inverse_float(lag_ref[...], inverse_ref[...]))


def local_corr(grad_ref, own_ref, skip_ref, forward_ref, inverse_ref, corr_ref, gained_ref, base_ref):
    first = lax.axis_index("context") == 0
    chans, tok = grad_ref.shape
    rows = GROUP * 8
    forward = forward_ref[...]
    inverse = inverse_ref[...]
    base_ref[...] = jnp.where(first, forward_float(own_ref[...], forward), 0.0)
    for start in range(0, chans, rows):
        span = pl.ds(start, rows)
        groups = pl.ds(start // GROUP, rows // GROUP)
        grad = grad_ref[span, :]
        spec = forward_exact(grad, forward)
        prod = conj_mul(group_spread(base_ref[groups, :]), spec)
        corr_ref[span, :] = inverse_float(jnp.concatenate(prod, axis=1), inverse)
        gain = jnp.broadcast_to(skip_ref[start // rows, :][None, :], (tok, rows)).T
        gained_ref[span, :] = gain * grad.astype(jnp.float32)


def late_core():
    return lax.axis_index("tensor") % 2 == 1


def before_swap_kernel(*refs):
    sources, (picked_ref, part_ref, lag_ref, taps_ref, corr_ref, gained_ref) = refs[:6], refs[6:12]
    base_ref, sems, *held = refs[12:]
    first = lax.axis_index("context") == 0
    copies = [pltpu.make_async_copy(*pair, sems.at[i]) for i, pair in enumerate(zip(sources, held))]

    def send(ref):
        copy = pltpu.make_async_copy(ref, picked_ref, sems.at[len(copies)])
        copy.start()
        copy.wait()

    @pl.when(late_core())
    def _():
        for batch in (copies[:1], copies[1:]):
            for copy in batch:
                copy.start()
            for copy in batch:
                copy.wait()
        in_ref, grad_ref, own_ref, skip_ref, forward_ref, inverse_ref = held
        picked_ref[...] = jnp.where(first, in_ref[...], grad_ref[...])
        local_lag(in_ref, grad_ref, forward_ref, inverse_ref, part_ref, lag_ref, taps_ref)
        local_corr(grad_ref, own_ref, skip_ref, forward_ref, inverse_ref, corr_ref, gained_ref, base_ref)

    @pl.when(jnp.logical_not(late_core()) & first)
    def _():
        send(sources[0])

    @pl.when(jnp.logical_not(late_core()) & jnp.logical_not(first))
    def _():
        send(sources[1])


def lag_after_kernel(in_ref, grad_ref, forward_ref, inverse_ref, *rest):
    part_ref, lag_ref, taps_ref = rest[3:]

    @pl.when(jnp.logical_not(late_core()))
    def _():
        local_lag(in_ref, grad_ref, forward_ref, inverse_ref, part_ref, lag_ref, taps_ref)


def corr_after_kernel(grad_ref, own_ref, skip_ref, forward_ref, inverse_ref, *rest):
    corr_ref, gained_ref, base_ref, held_ref, sem = rest[2:]

    @pl.when(jnp.logical_not(late_core()))
    def _():
        copy = pltpu.make_async_copy(skip_ref, held_ref, sem)
        copy.start()
        copy.wait()
        local_corr(grad_ref, own_ref, held_ref, forward_ref, inverse_ref, corr_ref, gained_ref, base_ref)


def cross_lag_kernel(moved_ref, part_ref, lag_ref, forward_ref, inverse_ref, out_ref, sum_ref):
    first = lax.axis_index("context") == 0
    chans, tok = moved_ref.shape
    rows = GROUP * 8
    forward = forward_ref[...]
    for start in range(0, chans, rows):
        span = pl.ds(start, rows)
        groups = pl.ds(start // GROUP, rows // GROUP)
        spec = forward_exact(moved_ref[span, :], forward)
        re, im = conj_mul(part_ref[span, :], spec)
        sum_ref[groups, :tok] = group_sum(re)
        sum_ref[groups, tok:] = group_sum(im)
    sign = sign_row(tok)
    re, im = sum_ref[:, :tok], sum_ref[:, tok:]
    total = jnp.concatenate(
        [
            jnp.where(first, lag_ref[:, :tok] + sign * im, re),
            jnp.where(first, lag_ref[:, tok:] - sign * re, -im),
        ],
        axis=1,
    )
    out_ref[...] = inverse_float(total, inverse_ref[...])


def cross_corr_kernel(
    moved_ref, grad_ref, own_ref, other_ref, corr_ref, gained_ref, forward_ref, inverse_ref, out_ref, turn_ref
):
    first = lax.axis_index("context") == 0
    chans, tok = moved_ref.shape
    rows = GROUP * 8
    forward = forward_ref[...]
    inverse = inverse_ref[...]
    own = forward_float(own_ref[...], forward)
    other = forward_float(other_ref[...], forward)
    sign = sign_row(tok)
    turn_ref[:, :tok] = other[:, :tok] - jnp.where(first, sign * own[:, tok:], 0.0)
    turn_ref[:, tok:] = other[:, tok:] + jnp.where(first, sign * own[:, :tok], 0.0)
    for start in range(0, chans, rows):
        span = pl.ds(start, rows)
        spec = forward_exact(jnp.where(first, moved_ref[span, :], grad_ref[span, :]), forward)
        turn = group_spread(turn_ref[pl.ds(start // GROUP, rows // GROUP), :])
        corr = corr_ref[span, :] + inverse_float(jnp.concatenate(conj_mul(turn, spec), axis=1), inverse)
        corr = corr.astype(jnp.bfloat16).astype(jnp.float32)
        out_ref[span, :] = (corr + gained_ref[span, :]).astype(jnp.bfloat16)


def store_kernel(held_ref, out_ref, sem):
    copy = pltpu.make_async_copy(held_ref, out_ref, sem)
    copy.start()
    copy.wait()


VMEM_SPEC = pl.BlockSpec(memory_space=pltpu.VMEM)


ANY_SPEC = pl.BlockSpec(memory_space=pl.ANY)


def call(kernel, out_shape, scratch, cost, *operands, in_specs=None, out_specs=None, aliases={}):
    return pl.pallas_call(
        kernel,
        out_shape=out_shape,
        in_specs=in_specs or [VMEM_SPEC] * len(operands),
        input_output_aliases=aliases,
        out_specs=out_specs or jax.tree.map(lambda _: VMEM_SPEC, out_shape),
        scratch_shapes=scratch,
        cost_estimate=pl.CostEstimate(flops=cost, bytes_accessed=cost // 256, transcendentals=0),
        compiler_params=pltpu.CompilerParams(vmem_limit_bytes=24 * 1024 * 1024),
    )(*operands)


def in_vmem(value):
    return pltpu.with_memory_space_constraint(value, pltpu.VMEM)


def paired(inputs, out_grad, filters, skip):
    chans, tok = inputs.shape[1:]
    groups = filters.shape[0]
    sequences = lax.axis_size("dp")
    swap = [(0, 1), (1, 0)]
    forward, inverse = block_tables(tok)
    own_in, own_grad = inputs[0], out_grad[0]
    skip_rows = skip.reshape(-1, GROUP * 8)
    cost = 4 * chans * tok * tok
    wide = pltpu.VMEM((chans, tok), jnp.float32)
    spectra = pltpu.VMEM((groups, 2 * tok), jnp.float32)

    work = (own_in, own_grad, filters, skip_rows, forward, inverse)
    results = (
        pltpu.VMEM((chans, 2 * tok), jnp.float32),
        spectra,
        pltpu.VMEM((groups, tok), jnp.float32),
        wide,
        wide,
    )
    picked, *held = call(
        before_swap_kernel,
        (pltpu.VMEM((chans, tok), jnp.bfloat16),) + results,
        [spectra, pltpu.SemaphoreType.DMA((len(work) + 1,))] + [pltpu.VMEM(v.shape, v.dtype) for v in work],
        cost,
        *(pltpu.with_memory_space_constraint(v, pltpu.HBM) for v in work),
        in_specs=[ANY_SPEC] * len(work),
    )
    moved = lax.ppermute(picked, "context", swap)
    part, lag, taps = call(
        lag_after_kernel,
        results[:3],
        [],
        8 * cost,
        own_in, own_grad, forward, inverse, *map(in_vmem, held[:3]),
        aliases={4: 0, 5: 1, 6: 2},
    )
    other_taps = lax.ppermute(taps, "context", swap)
    held = lax.optimization_barrier((part, *held[3:]))
    part = held[0]
    corr, gained = call(
        corr_after_kernel,
        results[3:],
        [spectra, pltpu.VMEM(skip_rows.shape, skip.dtype), pltpu.SemaphoreType.DMA],
        8 * cost,
        own_grad, filters, pltpu.with_memory_space_constraint(skip_rows, pltpu.HBM), forward, inverse,
        *map(in_vmem, held[1:]),
        in_specs=[VMEM_SPEC] * 2 + [ANY_SPEC] + [VMEM_SPEC] * 4,
        aliases={5: 0, 6: 1},
    )
    filters, part, corr = lax.optimization_barrier((filters, part, corr))
    other_filters = lax.ppermute(filters, "context", swap)
    total = other_taps + call(
        cross_lag_kernel,
        pltpu.VMEM((groups, tok), jnp.float32),
        [spectra],
        8 * cost,
        in_vmem(moved), part, lag, forward, inverse,
    )
    grad_input = call(
        cross_corr_kernel,
        pltpu.VMEM((chans, tok), jnp.bfloat16),
        [spectra],
        8 * cost,
        in_vmem(moved), own_grad, filters, in_vmem(other_filters), corr, gained, forward, inverse,
    )
    step = 1
    while step < sequences:
        total = total + lax.ppermute(total, "dp", [(i, i ^ step) for i in range(sequences)])
        total, grad_input = lax.optimization_barrier((total, grad_input))
        step *= 2
        if 2 * step == sequences:
            grad_input = call(
                store_kernel,
                jax.ShapeDtypeStruct((chans, tok), jnp.bfloat16),
                [pltpu.SemaphoreType.DMA],
                cost,
                in_vmem(grad_input),
                out_specs=ANY_SPEC,
            )
    norm_scale = 1.0 / math.sqrt(sequences * GROUP * 2 * tok)
    return (grad_input[None], total * norm_scale)


def dft_tables(size_one, size_two):
    padded_len = size_one * size_two
    range_one = jnp.arange(size_one, dtype=jnp.int32)
    range_two = jnp.arange(size_two, dtype=jnp.int32)
    angle_one = (range_one[:, None] * range_one[None, :] % size_one).astype(jnp.float32) * (
        -2.0 * math.pi / size_one
    )
    angle_two = (range_two[:, None] * range_two[None, :] % size_two).astype(jnp.float32) * (
        -2.0 * math.pi / size_two
    )
    angle_turn = (range_one[:, None] * range_two[None, :] % padded_len).astype(jnp.float32) * (
        -2.0 * math.pi / padded_len
    )
    return (
        jnp.cos(angle_one),
        jnp.sin(angle_one),
        jnp.cos(angle_two),
        jnp.sin(angle_two),
        jnp.cos(angle_turn),
        jnp.sin(angle_turn),
    )


def left_mul(matrix, operand):
    return jnp.einsum("kj,mjl->mkl", matrix, operand, precision=exact_mode)


def right_mul(operand, matrix):
    return jnp.einsum("mkj,jl->mkl", operand, matrix, precision=exact_mode)


def forward_real(signal, tables):
    one_re, one_im, two_re, two_im, turn_re, turn_im = tables
    half_rows = signal.shape[1]
    step_re = left_mul(one_re[:, :half_rows], signal)
    step_im = left_mul(one_im[:, :half_rows], signal)
    mid_re = step_re * turn_re - step_im * turn_im
    mid_im = step_re * turn_im + step_im * turn_re
    spec_re = right_mul(mid_re, two_re) - right_mul(mid_im, two_im)
    spec_im = right_mul(mid_re, two_im) + right_mul(mid_im, two_re)
    return (spec_re, spec_im)


def inverse_real(spec_re, spec_im, tables, half_rows):
    one_re, one_im, two_re, two_im, turn_re, turn_im = tables
    back_re = right_mul(spec_re, two_re) + right_mul(spec_im, two_im)
    back_im = right_mul(spec_im, two_re) - right_mul(spec_re, two_im)
    mid_re = back_re * turn_re + back_im * turn_im
    mid_im = back_im * turn_re - back_re * turn_im
    padded_len = one_re.shape[0] * two_re.shape[0]
    return (
        left_mul(one_re[:half_rows], mid_re) + left_mul(one_im[:half_rows], mid_im)
    ) / padded_len


def owner_groups(owners, own_ch, own_grp):
    starts = jnp.arange(owners, dtype=jnp.int32)[:, None] * own_ch // GROUP
    return starts + jnp.arange(own_grp, dtype=jnp.int32)[None, :]


def owned(inputs, out_grad, filters, skip):
    tok_dev = inputs.shape[2]
    ch_dev = inputs.shape[1]
    grp_dev = filters.shape[0]
    owners = lax.axis_size("context")
    seq_len = tok_dev * owners
    padded_len = 2 * seq_len
    own_ch = ch_dev // owners
    own_grp = max(1, own_ch // GROUP)
    per_group = own_ch // own_grp
    size_one = 1 << (padded_len.bit_length() - 1) // 2
    while padded_len % size_one != 0:
        size_one = size_one // 2
    size_two = padded_len // size_one
    half_rows = size_one // 2
    tables = dft_tables(size_one, size_two)
    moved_in, moved_grad = (
        lax.all_to_all(inputs, "context", split_axis=1, concat_axis=2, tiled=True),
        lax.all_to_all(out_grad, "context", split_axis=1, concat_axis=2, tiled=True),
    )
    slot_groups = owner_groups(owners, own_ch, own_grp)
    pick_rows = (
        slot_groups[:, :, None] == jnp.arange(grp_dev, dtype=jnp.int32)[None, None, :]
    ).astype(jnp.float32)
    outgoing = jnp.einsum("ojg,gt->ojt", pick_rows, filters, precision=exact_mode)
    own_filter = lax.all_to_all(
        outgoing, "context", split_axis=0, concat_axis=2, tiled=True
    ).reshape(own_grp, seq_len)
    sig_in = moved_in[0].astype(jnp.float32).reshape(own_ch, half_rows, size_two)
    sig_grad = moved_grad[0].astype(jnp.float32).reshape(own_ch, half_rows, size_two)
    in_re, in_im = forward_real(sig_in, tables)
    grad_re, grad_im = forward_real(sig_grad, tables)
    filt_re, filt_im = forward_real(own_filter.reshape(own_grp, half_rows, size_two), tables)
    grad_re4 = grad_re.reshape(own_grp, per_group, size_one, size_two)
    grad_im4 = grad_im.reshape(own_grp, per_group, size_one, size_two)
    filt_re4 = filt_re[:, None]
    filt_im4 = filt_im[:, None]
    prod_re = (filt_re4 * grad_re4 + filt_im4 * grad_im4).reshape(own_ch, size_one, size_two)
    prod_im = (filt_re4 * grad_im4 - filt_im4 * grad_re4).reshape(own_ch, size_one, size_two)
    correlated = (
        inverse_real(prod_re, prod_im, tables, half_rows)
        .reshape(1, own_ch, seq_len)
        .astype(jnp.bfloat16)
    )
    returned = lax.all_to_all(correlated, "context", split_axis=2, concat_axis=1, tiled=True)
    grad_input = (
        returned.astype(jnp.float32) + skip[None, :, None] * out_grad.astype(jnp.float32)
    ).astype(jnp.bfloat16)
    in_re4 = in_re.reshape(own_grp, per_group, size_one, size_two)
    in_im4 = in_im.reshape(own_grp, per_group, size_one, size_two)
    lag_re = (in_re4 * grad_re4 + in_im4 * grad_im4).sum(axis=1)
    lag_im = (in_re4 * grad_im4 - in_im4 * grad_re4).sum(axis=1)
    own_terms = inverse_real(lag_re, lag_im, tables, half_rows).reshape(own_grp, seq_len)
    pieces = lax.all_to_all(
        own_terms.reshape(own_grp, owners, tok_dev),
        "context",
        split_axis=1,
        concat_axis=0,
        tiled=True,
    )
    row_groups = owner_groups(owners, own_ch, own_grp).reshape(-1)
    pick_sum = (jnp.arange(grp_dev, dtype=jnp.int32)[:, None] == row_groups[None, :]).astype(
        jnp.float32
    )
    local_sum = jnp.dot(pick_sum, pieces.reshape(owners * own_grp, tok_dev), precision=exact_mode)
    summed = lax.psum(local_sum, "dp")
    norm_scale = 1.0 / math.sqrt(lax.axis_size("dp") * GROUP * seq_len)
    return (grad_input, summed * norm_scale)


def per_device(inputs, out_grad, filters, skip):
    sequences = lax.axis_size("dp")
    halves = lax.axis_size("context") == 2 and inputs.shape[0] == 1
    if halves and sequences & (sequences - 1) == 0 and inputs.shape[1] % (GROUP * 8) == 0:
        return paired(inputs, out_grad, filters, skip)
    return owned(inputs, out_grad, filters, skip)


def solution(mesh):
    in_specs = (
        P("dp", "tensor", "context"),
        P("dp", "tensor", "context"),
        P("tensor", "context"),
        P("tensor"),
    )
    out_specs = (P("dp", "tensor", "context"), P("tensor", "context"))
    return jax.shard_map(
        per_device, mesh=mesh, in_specs=in_specs, out_specs=out_specs, check_vma=False
    )
```

```python
import functools
import math

import jax
import jax.numpy as jnp
import numpy as np
from jax import lax
from jax.experimental import pallas as pl
from jax.experimental.pallas import tpu as pltpu
from jax.sharding import PartitionSpec as P

GROUP = 16


exact_mode = lax.Precision.HIGHEST


def block_tables(tok):
    step = np.arange(tok)
    angle = np.pi / tok * np.outer(step, step + 0.5)
    forward = np.concatenate([np.cos(angle), -np.sin(angle)], axis=1)
    inverse = np.concatenate([np.cos(angle).T, -np.sin(angle).T], axis=0) / tok
    pair = []
    for table, axis in ((forward, 0), (inverse, 1)):
        high = table.astype(jnp.bfloat16)
        low = (table - high.astype(np.float64)).astype(jnp.bfloat16)
        pair.append(jnp.asarray(np.concatenate([high, low], axis=axis)))
    return pair


def block_rows(chans):
    return math.gcd(chans // 2, GROUP * 32)


def matmul(left, right):
    return jnp.dot(left, right, preferred_element_type=jnp.float32)


def split(value):
    high = value.astype(jnp.bfloat16)
    return high, (value - high.astype(jnp.float32)).astype(jnp.bfloat16)


def forward_exact(block, forward):
    return matmul(jnp.concatenate([block, block], axis=1), forward)


def forward_float(value, forward):
    high, low = split(value)
    return forward_exact(high, forward) + matmul(low, forward[: value.shape[1]])


def inverse_float(spec, inverse):
    tok = spec.shape[1] // 2
    high, low = split(spec)
    both = matmul(high, inverse)
    return both[:, :tok] + both[:, tok:] + matmul(low, inverse[:, :tok])


def conj_mul(left, right):
    tok = left.shape[1] // 2
    left_re, left_im = left[:, :tok], left[:, tok:]
    right_re, right_im = right[:, :tok], right[:, tok:]
    return (
        left_re * right_re + left_im * right_im,
        left_re * right_im - left_im * right_re,
    )


def group_sum(value):
    rows, width = value.shape
    return value.reshape(rows // GROUP, GROUP, width).sum(axis=1)


def group_spread(value):
    rows, width = value.shape
    return jnp.broadcast_to(value[:, None, :], (rows, GROUP, width)).reshape(rows * GROUP, width)


def sign_row(tok):
    lane = lax.broadcasted_iota(jnp.int32, (1, tok), 1)
    return (1 - 2 * (lane % 2)).astype(jnp.float32)


def local_lag(in_ref, grad_ref, forward_ref, inverse_ref, part_ref, lag_ref, taps_ref):
    first = lax.axis_index("context") == 0
    chans, tok = in_ref.shape
    rows = block_rows(chans)
    forward = forward_ref[...]
    for start in range(0, chans, rows):
        span = pl.ds(start, rows)
        groups = pl.ds(start // GROUP, rows // GROUP)
        in_spec = forward_exact(in_ref[span, :], forward)
        grad_spec = forward_exact(grad_ref[span, :], forward)
        lag_re, lag_im = conj_mul(in_spec, grad_spec)
        lag_ref[groups, :tok] = group_sum(lag_re)
        lag_ref[groups, tok:] = group_sum(lag_im)
        part_ref[span, :] = jnp.where(first, in_spec, grad_spec)
    taps_ref[...] = jnp.where(first, 0.0, inverse_float(lag_ref[...], inverse_ref[...]))


def local_corr(grad_ref, own_ref, skip_ref, forward_ref, inverse_ref, corr_ref, gained_ref, base_ref):
    first = lax.axis_index("context") == 0
    chans, tok = grad_ref.shape
    rows = block_rows(chans)
    forward = forward_ref[...]
    inverse = inverse_ref[...]
    base_ref[...] = jnp.where(first, forward_float(own_ref[...], forward), 0.0)
    for start in range(0, chans, rows):
        span = pl.ds(start, rows)
        groups = pl.ds(start // GROUP, rows // GROUP)
        grad = grad_ref[span, :]
        spec = forward_exact(grad, forward)
        prod = conj_mul(group_spread(base_ref[groups, :]), spec)
        corr_ref[span, :] = inverse_float(jnp.concatenate(prod, axis=1), inverse)
        for at in range(0, rows, tok):
            gain = jnp.broadcast_to(skip_ref[(start + at) // tok, :][None, :], (tok, tok)).T
            gained_ref[pl.ds(start + at, tok), :] = gain * grad[at : at + tok, :].astype(jnp.float32)


def load_kernel(in_ref, grad_ref, filters_ref, skip_ref, *refs):
    first = lax.axis_index("context") == 0
    *parts, in_held, grad_held, filters_held, skip_held, sems = refs
    pairs = ((in_ref, in_held), (grad_ref, grad_held), (filters_ref, filters_held), (skip_ref, skip_held))
    copies = [pltpu.make_async_copy(*pair, sems.at[i]) for i, pair in enumerate(pairs)]
    for copy in copies:
        copy.start()
    for copy in copies:
        copy.wait()
    start = 0
    for part in parts:
        span = pl.ds(start, part.shape[0])
        part[...] = jnp.where(first, in_held[span, :], grad_held[span, :])
        start += part.shape[0]


def moved_block(parts, start, rows):
    for part in parts:
        if start < part.shape[0]:
            return part[pl.ds(start, rows), :]
        start -= part.shape[0]


def cross_lag_kernel(*refs):
    *parts, part_ref, lag_ref, forward_ref, inverse_ref, out_ref, sum_ref = refs
    first = lax.axis_index("context") == 0
    chans, tok = part_ref.shape[0], out_ref.shape[1]
    rows = block_rows(chans)
    forward = forward_ref[...]
    for start in range(0, chans, rows):
        span = pl.ds(start, rows)
        groups = pl.ds(start // GROUP, rows // GROUP)
        spec = forward_exact(moved_block(parts, start, rows), forward)
        re, im = conj_mul(part_ref[span, :], spec)
        sum_ref[groups, :tok] = group_sum(re)
        sum_ref[groups, tok:] = group_sum(im)
    sign = sign_row(tok)
    re, im = sum_ref[:, :tok], sum_ref[:, tok:]
    total = jnp.concatenate(
        [
            jnp.where(first, lag_ref[:, :tok] + sign * im, re),
            jnp.where(first, lag_ref[:, tok:] - sign * re, -im),
        ],
        axis=1,
    )
    out_ref[...] = inverse_float(total, inverse_ref[...])


def cross_corr_kernel(*refs):
    *parts, grad_ref, own_ref, other_ref, corr_ref, gained_ref, forward_ref, inverse_ref, out_ref, turn_ref = refs
    first = lax.axis_index("context") == 0
    chans, tok = grad_ref.shape
    rows = block_rows(chans)
    forward = forward_ref[...]
    inverse = inverse_ref[...]
    own = forward_float(own_ref[...], forward)
    other = forward_float(other_ref[...], forward)
    sign = sign_row(tok)
    turn_ref[:, :tok] = other[:, :tok] - jnp.where(first, sign * own[:, tok:], 0.0)
    turn_ref[:, tok:] = other[:, tok:] + jnp.where(first, sign * own[:, :tok], 0.0)
    for start in range(0, chans, rows):
        span = pl.ds(start, rows)
        spec = forward_exact(jnp.where(first, moved_block(parts, start, rows), grad_ref[span, :]), forward)
        turn = group_spread(turn_ref[pl.ds(start // GROUP, rows // GROUP), :])
        corr = corr_ref[span, :] + inverse_float(jnp.concatenate(conj_mul(turn, spec), axis=1), inverse)
        corr = corr.astype(jnp.bfloat16).astype(jnp.float32)
        out_ref[span, :] = (corr + gained_ref[span, :]).astype(jnp.bfloat16)


def finish_kernel(scale, left_ref, right_ref, out_ref):
    out_ref[...] = (left_ref[...] + right_ref[...]) * scale


def store_kernel(held_ref, out_ref, sem):
    copy = pltpu.make_async_copy(held_ref, out_ref, sem)
    copy.start()
    copy.wait()


VMEM_SPEC = pl.BlockSpec(memory_space=pltpu.VMEM)


ANY_SPEC = pl.BlockSpec(memory_space=pl.ANY)


def call(kernel, out_shape, scratch, cost, *operands, in_specs=None, out_specs=None, aliases={}):
    return pl.pallas_call(
        kernel,
        out_shape=out_shape,
        in_specs=in_specs or [VMEM_SPEC] * len(operands),
        input_output_aliases=aliases,
        out_specs=out_specs or jax.tree.map(lambda _: VMEM_SPEC, out_shape),
        scratch_shapes=scratch,
        cost_estimate=pl.CostEstimate(flops=cost, bytes_accessed=cost // 256, transcendentals=0),
        compiler_params=pltpu.CompilerParams(vmem_limit_bytes=24 * 1024 * 1024),
    )(*operands)


def in_vmem(value):
    return pltpu.with_memory_space_constraint(value, pltpu.VMEM)


def paired(late, inputs, out_grad, filters, skip):
    chans, tok = inputs.shape[1:]
    groups = filters.shape[0]
    sequences = lax.axis_size("dp")
    swap = [(0, 1), (1, 0)]
    forward, inverse = block_tables(tok)
    own_in, own_grad = inputs[0], out_grad[0]
    skip_rows = skip.reshape(-1, tok)
    cost = 4 * chans * tok * tok
    wide = pltpu.VMEM((chans, tok), jnp.float32)
    spectra = pltpu.VMEM((groups, 2 * tok), jnp.float32)

    rows = block_rows(chans)
    cut = chans // (2 * rows) * rows
    block = pltpu.VMEM((chans, tok), jnp.bfloat16)
    narrow = pltpu.VMEM((groups, tok), jnp.float32)
    sizes = (cut, chans - cut) if late else (chans,)
    parts = tuple(pltpu.VMEM((size, tok), jnp.bfloat16) for size in sizes)
    loaded = call(
        load_kernel,
        parts + (block, block, narrow, pltpu.VMEM(skip_rows.shape, jnp.float32)),
        [pltpu.SemaphoreType.DMA((4,))],
        cost,
        *(pltpu.with_memory_space_constraint(v, pltpu.HBM) for v in (own_in, own_grad, filters, skip_rows)),
        in_specs=[ANY_SPEC] * 4,
    )
    own_in, own_grad, own, skip_held = loaded[-4:]
    moved = [lax.ppermute(loaded[0], "context", swap)]
    part, lag, taps = call(
        local_lag,
        (pltpu.VMEM((chans, 2 * tok), jnp.float32), spectra, narrow),
        [],
        8 * cost,
        own_in, own_grad, forward, inverse,
    )

    def correlate_local(grad):
        return call(local_corr, (wide, wide), [spectra], 8 * cost, grad, own, skip_held, forward, inverse)

    if late:
        corr, gained = correlate_local(own_grad)
        moved[0], rest, taps, part, own = lax.optimization_barrier((moved[0], loaded[1], taps, part, own, corr))[:5]
        moved.append(lax.ppermute(rest, "context", swap))
        taps, own = lax.optimization_barrier((taps, own))
    other_taps = lax.ppermute(taps, "context", swap)
    if not late:
        corr, gained = correlate_local(own_grad)
        own, part, corr = lax.optimization_barrier((own, part, corr))
    other_filters = lax.ppermute(own, "context", swap)
    total = other_taps + call(
        cross_lag_kernel,
        narrow,
        [spectra],
        8 * cost,
        *map(in_vmem, moved), part, lag, forward, inverse,
    )

    def correlate(filters):
        return call(
            cross_corr_kernel,
            pltpu.VMEM((chans, tok), jnp.bfloat16),
            [spectra],
            8 * cost,
            *map(in_vmem, moved), own_grad, own, in_vmem(filters), corr, gained, forward, inverse,
        )

    norm_scale = 1.0 / math.sqrt(sequences * GROUP * 2 * tok)
    got, step = jnp.zeros_like(total), 1
    grad_input = correlate(other_filters) if late else None
    while step < sequences:
        got = lax.ppermute(total, "dp", [(i, i ^ step) for i in range(sequences)])
        step *= 2
        if step < sequences:
            if late:
                got, grad_input = lax.optimization_barrier((got, grad_input))
            else:
                got, corr = lax.optimization_barrier((got, corr))
            total = total + got
    if not late:
        grad_input = correlate(other_filters)
    stored = call(
        store_kernel,
        jax.ShapeDtypeStruct((chans, tok), jnp.bfloat16),
        [pltpu.SemaphoreType.DMA],
        cost,
        in_vmem(grad_input),
        out_specs=ANY_SPEC,
    )
    got, _ = lax.optimization_barrier((got, stored))
    grad_filter = call(
        functools.partial(finish_kernel, norm_scale),
        jax.ShapeDtypeStruct((groups, tok), jnp.float32),
        [],
        cost,
        total, got,
    )
    return (stored[None], grad_filter)


def dft_tables(size_one, size_two):
    padded_len = size_one * size_two
    range_one = jnp.arange(size_one, dtype=jnp.int32)
    range_two = jnp.arange(size_two, dtype=jnp.int32)
    angle_one = (range_one[:, None] * range_one[None, :] % size_one).astype(jnp.float32) * (
        -2.0 * math.pi / size_one
    )
    angle_two = (range_two[:, None] * range_two[None, :] % size_two).astype(jnp.float32) * (
        -2.0 * math.pi / size_two
    )
    angle_turn = (range_one[:, None] * range_two[None, :] % padded_len).astype(jnp.float32) * (
        -2.0 * math.pi / padded_len
    )
    return (
        jnp.cos(angle_one),
        jnp.sin(angle_one),
        jnp.cos(angle_two),
        jnp.sin(angle_two),
        jnp.cos(angle_turn),
        jnp.sin(angle_turn),
    )


def left_mul(matrix, operand):
    return jnp.einsum("kj,mjl->mkl", matrix, operand, precision=exact_mode)


def right_mul(operand, matrix):
    return jnp.einsum("mkj,jl->mkl", operand, matrix, precision=exact_mode)


def forward_real(signal, tables):
    one_re, one_im, two_re, two_im, turn_re, turn_im = tables
    half_rows = signal.shape[1]
    step_re = left_mul(one_re[:, :half_rows], signal)
    step_im = left_mul(one_im[:, :half_rows], signal)
    mid_re = step_re * turn_re - step_im * turn_im
    mid_im = step_re * turn_im + step_im * turn_re
    spec_re = right_mul(mid_re, two_re) - right_mul(mid_im, two_im)
    spec_im = right_mul(mid_re, two_im) + right_mul(mid_im, two_re)
    return (spec_re, spec_im)


def inverse_real(spec_re, spec_im, tables, half_rows):
    one_re, one_im, two_re, two_im, turn_re, turn_im = tables
    back_re = right_mul(spec_re, two_re) + right_mul(spec_im, two_im)
    back_im = right_mul(spec_im, two_re) - right_mul(spec_re, two_im)
    mid_re = back_re * turn_re + back_im * turn_im
    mid_im = back_im * turn_re - back_re * turn_im
    padded_len = one_re.shape[0] * two_re.shape[0]
    return (
        left_mul(one_re[:half_rows], mid_re) + left_mul(one_im[:half_rows], mid_im)
    ) / padded_len


def owner_groups(owners, own_ch, own_grp):
    starts = jnp.arange(owners, dtype=jnp.int32)[:, None] * own_ch // GROUP
    return starts + jnp.arange(own_grp, dtype=jnp.int32)[None, :]


def owned(inputs, out_grad, filters, skip):
    tok_dev = inputs.shape[2]
    ch_dev = inputs.shape[1]
    grp_dev = filters.shape[0]
    owners = lax.axis_size("context")
    seq_len = tok_dev * owners
    padded_len = 2 * seq_len
    own_ch = ch_dev // owners
    own_grp = max(1, own_ch // GROUP)
    per_group = own_ch // own_grp
    size_one = 1 << (padded_len.bit_length() - 1) // 2
    while padded_len % size_one != 0:
        size_one = size_one // 2
    size_two = padded_len // size_one
    half_rows = size_one // 2
    tables = dft_tables(size_one, size_two)
    moved_in, moved_grad = (
        lax.all_to_all(inputs, "context", split_axis=1, concat_axis=2, tiled=True),
        lax.all_to_all(out_grad, "context", split_axis=1, concat_axis=2, tiled=True),
    )
    slot_groups = owner_groups(owners, own_ch, own_grp)
    pick_rows = (
        slot_groups[:, :, None] == jnp.arange(grp_dev, dtype=jnp.int32)[None, None, :]
    ).astype(jnp.float32)
    outgoing = jnp.einsum("ojg,gt->ojt", pick_rows, filters, precision=exact_mode)
    own_filter = lax.all_to_all(
        outgoing, "context", split_axis=0, concat_axis=2, tiled=True
    ).reshape(own_grp, seq_len)
    sig_in = moved_in[0].astype(jnp.float32).reshape(own_ch, half_rows, size_two)
    sig_grad = moved_grad[0].astype(jnp.float32).reshape(own_ch, half_rows, size_two)
    in_re, in_im = forward_real(sig_in, tables)
    grad_re, grad_im = forward_real(sig_grad, tables)
    filt_re, filt_im = forward_real(own_filter.reshape(own_grp, half_rows, size_two), tables)
    grad_re4 = grad_re.reshape(own_grp, per_group, size_one, size_two)
    grad_im4 = grad_im.reshape(own_grp, per_group, size_one, size_two)
    filt_re4 = filt_re[:, None]
    filt_im4 = filt_im[:, None]
    prod_re = (filt_re4 * grad_re4 + filt_im4 * grad_im4).reshape(own_ch, size_one, size_two)
    prod_im = (filt_re4 * grad_im4 - filt_im4 * grad_re4).reshape(own_ch, size_one, size_two)
    correlated = (
        inverse_real(prod_re, prod_im, tables, half_rows)
        .reshape(1, own_ch, seq_len)
        .astype(jnp.bfloat16)
    )
    returned = lax.all_to_all(correlated, "context", split_axis=2, concat_axis=1, tiled=True)
    grad_input = (
        returned.astype(jnp.float32) + skip[None, :, None] * out_grad.astype(jnp.float32)
    ).astype(jnp.bfloat16)
    in_re4 = in_re.reshape(own_grp, per_group, size_one, size_two)
    in_im4 = in_im.reshape(own_grp, per_group, size_one, size_two)
    lag_re = (in_re4 * grad_re4 + in_im4 * grad_im4).sum(axis=1)
    lag_im = (in_re4 * grad_im4 - in_im4 * grad_re4).sum(axis=1)
    own_terms = inverse_real(lag_re, lag_im, tables, half_rows).reshape(own_grp, seq_len)
    pieces = lax.all_to_all(
        own_terms.reshape(own_grp, owners, tok_dev),
        "context",
        split_axis=1,
        concat_axis=0,
        tiled=True,
    )
    row_groups = owner_groups(owners, own_ch, own_grp).reshape(-1)
    pick_sum = (jnp.arange(grp_dev, dtype=jnp.int32)[:, None] == row_groups[None, :]).astype(
        jnp.float32
    )
    local_sum = jnp.dot(pick_sum, pieces.reshape(owners * own_grp, tok_dev), precision=exact_mode)
    summed = lax.psum(local_sum, "dp")
    norm_scale = 1.0 / math.sqrt(lax.axis_size("dp") * GROUP * seq_len)
    return (grad_input, summed * norm_scale)


def per_device(inputs, out_grad, filters, skip):
    sequences = lax.axis_size("dp")
    halves = lax.axis_size("context") == 2 and inputs.shape[0] == 1
    if halves and sequences & (sequences - 1) == 0 and inputs.shape[1] % (2 * inputs.shape[2]) == 0:
        late = lax.axis_index("tensor") % 2 == 1
        return lax.cond(
            late, functools.partial(paired, True), functools.partial(paired, False), inputs, out_grad, filters, skip
        )
    return owned(inputs, out_grad, filters, skip)


def solution(mesh):
    in_specs = (
        P("dp", "tensor", "context"),
        P("dp", "tensor", "context"),
        P("tensor", "context"),
        P("tensor"),
    )
    out_specs = (P("dp", "tensor", "context"), P("tensor", "context"))
    return jax.shard_map(
        per_device, mesh=mesh, in_specs=in_specs, out_specs=out_specs, check_vma=False
    )
```

```python
import functools
import math

import jax
import jax.numpy as jnp
import numpy as np
from jax import lax
from jax.experimental import pallas as pl
from jax.experimental.pallas import tpu as pltpu
from jax.sharding import PartitionSpec as P

GROUP = 16


exact_mode = lax.Precision.HIGHEST


def block_tables(tok):
    step = np.arange(tok)
    angle = np.pi / tok * np.outer(step, step + 0.5)
    forward = np.concatenate([np.cos(angle), -np.sin(angle)], axis=1)
    inverse = np.concatenate([np.cos(angle).T, -np.sin(angle).T], axis=0) / tok
    pair = []
    for table, axis in ((forward, 0), (inverse, 1)):
        high = table.astype(jnp.bfloat16)
        low = (table - high.astype(np.float64)).astype(jnp.bfloat16)
        pair.append(jnp.asarray(np.concatenate([high, low], axis=axis)))
    return pair


def block_rows(chans):
    return math.gcd(chans // 2, GROUP * 32)


def matmul(left, right):
    return jnp.dot(left, right, preferred_element_type=jnp.float32)


def split(value):
    high = value.astype(jnp.bfloat16)
    return high, (value - high.astype(jnp.float32)).astype(jnp.bfloat16)


def forward_exact(block, forward):
    return matmul(jnp.concatenate([block, block], axis=1), forward)


def forward_float(value, forward):
    high, low = split(value)
    return forward_exact(high, forward) + matmul(low, forward[: value.shape[1]])


def inverse_float(spec, inverse):
    tok = spec.shape[1] // 2
    high, low = split(spec)
    both = matmul(high, inverse)
    return both[:, :tok] + both[:, tok:] + matmul(low, inverse[:, :tok])


def conj_mul(left, right):
    tok = left.shape[1] // 2
    left_re, left_im = left[:, :tok], left[:, tok:]
    right_re, right_im = right[:, :tok], right[:, tok:]
    return (
        left_re * right_re + left_im * right_im,
        left_re * right_im - left_im * right_re,
    )


def group_sum(value):
    rows, width = value.shape
    return value.reshape(rows // GROUP, GROUP, width).sum(axis=1)


def group_spread(value):
    rows, width = value.shape
    return jnp.broadcast_to(value[:, None, :], (rows, GROUP, width)).reshape(rows * GROUP, width)


def sign_row(tok):
    lane = lax.broadcasted_iota(jnp.int32, (1, tok), 1)
    return (1 - 2 * (lane % 2)).astype(jnp.float32)


def local_lag(in_ref, grad_ref, forward_ref, inverse_ref, part_ref, kept_ref, taps_ref, lag_ref):
    first = lax.axis_index("context") == 0
    chans, tok = in_ref.shape
    rows = block_rows(chans)
    forward = forward_ref[...]
    for start in range(0, chans, rows):
        span = pl.ds(start, rows)
        groups = pl.ds(start // GROUP, rows // GROUP)
        in_spec = forward_exact(in_ref[span, :], forward)
        grad_spec = forward_exact(grad_ref[span, :], forward)
        lag_re, lag_im = conj_mul(in_spec, grad_spec)
        lag_ref[groups, :tok] = group_sum(lag_re)
        lag_ref[groups, tok:] = group_sum(lag_im)
        part_ref[span, :] = jnp.where(first, in_spec, grad_spec)
    taps = inverse_float(lag_ref[...], inverse_ref[...])
    kept_ref[...] = jnp.where(first, taps, 0.0)
    taps_ref[...] = jnp.where(first, 0.0, taps)


def local_corr(grad_ref, own_ref, skip_ref, forward_ref, inverse_ref, corr_ref, gained_ref, base_ref):
    first = lax.axis_index("context") == 0
    chans, tok = grad_ref.shape
    rows = block_rows(chans)
    forward = forward_ref[...]
    inverse = inverse_ref[...]
    base_ref[...] = jnp.where(first, forward_float(own_ref[...], forward), 0.0)
    for start in range(0, chans, rows):
        span = pl.ds(start, rows)
        groups = pl.ds(start // GROUP, rows // GROUP)
        grad = grad_ref[span, :]
        spec = forward_exact(grad, forward)
        prod = conj_mul(group_spread(base_ref[groups, :]), spec)
        corr_ref[span, :] = inverse_float(jnp.concatenate(prod, axis=1), inverse)
        for at in range(0, rows, tok):
            gain = jnp.broadcast_to(skip_ref[(start + at) // tok, :][None, :], (tok, tok)).T
            gained_ref[pl.ds(start + at, tok), :] = gain * grad[at : at + tok, :].astype(jnp.float32)


def load_kernel(in_ref, grad_ref, filters_ref, skip_ref, *refs):
    first = lax.axis_index("context") == 0
    *parts, in_held, grad_held, filters_held, skip_held, sems = refs
    pairs = ((in_ref, in_held), (grad_ref, grad_held), (filters_ref, filters_held), (skip_ref, skip_held))
    copies = [pltpu.make_async_copy(*pair, sems.at[i]) for i, pair in enumerate(pairs)]
    for copy in copies:
        copy.start()
    for copy in copies:
        copy.wait()
    start = 0
    for part in parts:
        span = pl.ds(start, part.shape[0])
        part[...] = jnp.where(first, in_held[span, :], grad_held[span, :])
        start += part.shape[0]


def moved_block(parts, start, rows):
    for part in parts:
        if start < part.shape[0]:
            return part[pl.ds(start, rows), :]
        start -= part.shape[0]


def cross_lag_kernel(*refs):
    *parts, part_ref, forward_ref, inverse_ref, out_ref, sum_ref = refs
    first = lax.axis_index("context") == 0
    chans, tok = part_ref.shape[0], out_ref.shape[1]
    rows = block_rows(chans)
    forward = forward_ref[...]
    for start in range(0, chans, rows):
        span = pl.ds(start, rows)
        groups = pl.ds(start // GROUP, rows // GROUP)
        spec = forward_exact(moved_block(parts, start, rows), forward)
        re, im = conj_mul(part_ref[span, :], spec)
        sum_ref[groups, :tok] = group_sum(re)
        sum_ref[groups, tok:] = group_sum(im)
    sign = sign_row(tok)
    re, im = sum_ref[:, :tok], sum_ref[:, tok:]
    total = jnp.concatenate(
        [
            jnp.where(first, sign * im, re),
            -jnp.where(first, sign * re, im),
        ],
        axis=1,
    )
    out_ref[...] = inverse_float(total, inverse_ref[...])


def cross_corr_kernel(*refs):
    *parts, grad_ref, own_ref, other_ref, corr_ref, gained_ref, forward_ref, inverse_ref, out_ref, turn_ref = refs
    first = lax.axis_index("context") == 0
    chans, tok = grad_ref.shape
    rows = block_rows(chans)
    forward = forward_ref[...]
    inverse = inverse_ref[...]
    own = forward_float(own_ref[...], forward)
    other = forward_float(other_ref[...], forward)
    sign = sign_row(tok)
    turn_ref[:, :tok] = other[:, :tok] - jnp.where(first, sign * own[:, tok:], 0.0)
    turn_ref[:, tok:] = other[:, tok:] + jnp.where(first, sign * own[:, :tok], 0.0)
    for start in range(0, chans, rows):
        span = pl.ds(start, rows)
        spec = forward_exact(jnp.where(first, moved_block(parts, start, rows), grad_ref[span, :]), forward)
        turn = group_spread(turn_ref[pl.ds(start // GROUP, rows // GROUP), :])
        corr = corr_ref[span, :] + inverse_float(jnp.concatenate(conj_mul(turn, spec), axis=1), inverse)
        corr = corr.astype(jnp.bfloat16).astype(jnp.float32)
        out_ref[span, :] = (corr + gained_ref[span, :]).astype(jnp.bfloat16)


def finish_kernel(scale, left_ref, right_ref, out_ref):
    out_ref[...] = (left_ref[...] + right_ref[...]) * scale


def store_kernel(held_ref, out_ref, sem):
    copy = pltpu.make_async_copy(held_ref, out_ref, sem)
    copy.start()
    copy.wait()


VMEM_SPEC = pl.BlockSpec(memory_space=pltpu.VMEM)


ANY_SPEC = pl.BlockSpec(memory_space=pl.ANY)


def call(kernel, out_shape, scratch, cost, *operands, in_specs=None, out_specs=None, aliases={}):
    return pl.pallas_call(
        kernel,
        out_shape=out_shape,
        in_specs=in_specs or [VMEM_SPEC] * len(operands),
        input_output_aliases=aliases,
        out_specs=out_specs or jax.tree.map(lambda _: VMEM_SPEC, out_shape),
        scratch_shapes=scratch,
        cost_estimate=pl.CostEstimate(flops=cost, bytes_accessed=cost // 256, transcendentals=0),
        compiler_params=pltpu.CompilerParams(vmem_limit_bytes=24 * 1024 * 1024),
    )(*operands)


def in_vmem(value):
    return pltpu.with_memory_space_constraint(value, pltpu.VMEM)


def paired(late, inputs, out_grad, filters, skip):
    chans, tok = inputs.shape[1:]
    groups = filters.shape[0]
    sequences = lax.axis_size("dp")
    swap = [(0, 1), (1, 0)]
    forward, inverse = block_tables(tok)
    own_in, own_grad = inputs[0], out_grad[0]
    skip_rows = skip.reshape(-1, tok)
    cost = 4 * chans * tok * tok
    wide = pltpu.VMEM((chans, tok), jnp.float32)
    spectra = pltpu.VMEM((groups, 2 * tok), jnp.float32)

    rows = block_rows(chans)
    cut = chans // (2 * rows) * rows
    block = pltpu.VMEM((chans, tok), jnp.bfloat16)
    narrow = pltpu.VMEM((groups, tok), jnp.float32)
    sizes = (cut, chans - cut) if late else (chans,)
    parts = tuple(pltpu.VMEM((size, tok), jnp.bfloat16) for size in sizes)
    loaded = call(
        load_kernel,
        parts + (block, block, narrow, pltpu.VMEM(skip_rows.shape, jnp.float32)),
        [pltpu.SemaphoreType.DMA((4,))],
        cost,
        *(pltpu.with_memory_space_constraint(v, pltpu.HBM) for v in (own_in, own_grad, filters, skip_rows)),
        in_specs=[ANY_SPEC] * 4,
    )
    own_in, own_grad, own, skip_held = loaded[-4:]
    moved = [lax.ppermute(loaded[0], "context", swap)]
    part, kept, taps = call(
        local_lag,
        (pltpu.VMEM((chans, 2 * tok), jnp.float32), narrow, narrow),
        [spectra],
        8 * cost,
        own_in, own_grad, forward, inverse,
    )

    def correlate_local(grad):
        return call(local_corr, (wide, wide), [spectra], 8 * cost, grad, own, skip_held, forward, inverse)

    if late:
        corr, gained = correlate_local(own_grad)
        moved[0], rest, taps, part, own = lax.optimization_barrier((moved[0], loaded[1], taps, part, own, corr))[:5]
        moved.append(lax.ppermute(rest, "context", swap))
        taps, own = lax.optimization_barrier((taps, own))
    other_taps = lax.ppermute(taps, "context", swap)
    if not late:
        corr, gained = correlate_local(own_grad)
        own, part, corr = lax.optimization_barrier((own, part, corr))
    other_filters = lax.ppermute(own, "context", swap)
    total = (kept + other_taps) + call(
        cross_lag_kernel,
        narrow,
        [spectra],
        8 * cost,
        *map(in_vmem, moved), part, forward, inverse,
    )

    def correlate(filters):
        return call(
            cross_corr_kernel,
            pltpu.VMEM((chans, tok), jnp.bfloat16),
            [spectra],
            8 * cost,
            *map(in_vmem, moved), own_grad, own, in_vmem(filters), corr, gained, forward, inverse,
        )

    norm_scale = 1.0 / math.sqrt(sequences * GROUP * 2 * tok)
    got, step = jnp.zeros_like(total), 1
    grad_input = correlate(other_filters) if late else None
    while step < sequences:
        got = lax.ppermute(total, "dp", [(i, i ^ step) for i in range(sequences)])
        step *= 2
        if step < sequences:
            if late:
                got, grad_input = lax.optimization_barrier((got, grad_input))
            else:
                got, corr = lax.optimization_barrier((got, corr))
            total = total + got
    if not late:
        grad_input = correlate(other_filters)
    stored = call(
        store_kernel,
        jax.ShapeDtypeStruct((chans, tok), jnp.bfloat16),
        [pltpu.SemaphoreType.DMA],
        cost,
        in_vmem(grad_input),
        out_specs=ANY_SPEC,
    )
    got, _ = lax.optimization_barrier((got, stored))
    grad_filter = call(
        functools.partial(finish_kernel, norm_scale),
        jax.ShapeDtypeStruct((groups, tok), jnp.float32),
        [],
        cost,
        total, got,
    )
    return (stored[None], grad_filter)


def dft_tables(size_one, size_two):
    padded_len = size_one * size_two
    range_one = jnp.arange(size_one, dtype=jnp.int32)
    range_two = jnp.arange(size_two, dtype=jnp.int32)
    angle_one = (range_one[:, None] * range_one[None, :] % size_one).astype(jnp.float32) * (
        -2.0 * math.pi / size_one
    )
    angle_two = (range_two[:, None] * range_two[None, :] % size_two).astype(jnp.float32) * (
        -2.0 * math.pi / size_two
    )
    angle_turn = (range_one[:, None] * range_two[None, :] % padded_len).astype(jnp.float32) * (
        -2.0 * math.pi / padded_len
    )
    return (
        jnp.cos(angle_one),
        jnp.sin(angle_one),
        jnp.cos(angle_two),
        jnp.sin(angle_two),
        jnp.cos(angle_turn),
        jnp.sin(angle_turn),
    )


def left_mul(matrix, operand):
    return jnp.einsum("kj,mjl->mkl", matrix, operand, precision=exact_mode)


def right_mul(operand, matrix):
    return jnp.einsum("mkj,jl->mkl", operand, matrix, precision=exact_mode)


def forward_real(signal, tables):
    one_re, one_im, two_re, two_im, turn_re, turn_im = tables
    half_rows = signal.shape[1]
    step_re = left_mul(one_re[:, :half_rows], signal)
    step_im = left_mul(one_im[:, :half_rows], signal)
    mid_re = step_re * turn_re - step_im * turn_im
    mid_im = step_re * turn_im + step_im * turn_re
    spec_re = right_mul(mid_re, two_re) - right_mul(mid_im, two_im)
    spec_im = right_mul(mid_re, two_im) + right_mul(mid_im, two_re)
    return (spec_re, spec_im)


def inverse_real(spec_re, spec_im, tables, half_rows):
    one_re, one_im, two_re, two_im, turn_re, turn_im = tables
    back_re = right_mul(spec_re, two_re) + right_mul(spec_im, two_im)
    back_im = right_mul(spec_im, two_re) - right_mul(spec_re, two_im)
    mid_re = back_re * turn_re + back_im * turn_im
    mid_im = back_im * turn_re - back_re * turn_im
    padded_len = one_re.shape[0] * two_re.shape[0]
    return (
        left_mul(one_re[:half_rows], mid_re) + left_mul(one_im[:half_rows], mid_im)
    ) / padded_len


def owner_groups(owners, own_ch, own_grp):
    starts = jnp.arange(owners, dtype=jnp.int32)[:, None] * own_ch // GROUP
    return starts + jnp.arange(own_grp, dtype=jnp.int32)[None, :]


def owned(inputs, out_grad, filters, skip):
    tok_dev = inputs.shape[2]
    ch_dev = inputs.shape[1]
    grp_dev = filters.shape[0]
    owners = lax.axis_size("context")
    seq_len = tok_dev * owners
    padded_len = 2 * seq_len
    own_ch = ch_dev // owners
    own_grp = max(1, own_ch // GROUP)
    per_group = own_ch // own_grp
    size_one = 1 << (padded_len.bit_length() - 1) // 2
    while padded_len % size_one != 0:
        size_one = size_one // 2
    size_two = padded_len // size_one
    half_rows = size_one // 2
    tables = dft_tables(size_one, size_two)
    moved_in, moved_grad = (
        lax.all_to_all(inputs, "context", split_axis=1, concat_axis=2, tiled=True),
        lax.all_to_all(out_grad, "context", split_axis=1, concat_axis=2, tiled=True),
    )
    slot_groups = owner_groups(owners, own_ch, own_grp)
    pick_rows = (
        slot_groups[:, :, None] == jnp.arange(grp_dev, dtype=jnp.int32)[None, None, :]
    ).astype(jnp.float32)
    outgoing = jnp.einsum("ojg,gt->ojt", pick_rows, filters, precision=exact_mode)
    own_filter = lax.all_to_all(
        outgoing, "context", split_axis=0, concat_axis=2, tiled=True
    ).reshape(own_grp, seq_len)
    sig_in = moved_in[0].astype(jnp.float32).reshape(own_ch, half_rows, size_two)
    sig_grad = moved_grad[0].astype(jnp.float32).reshape(own_ch, half_rows, size_two)
    in_re, in_im = forward_real(sig_in, tables)
    grad_re, grad_im = forward_real(sig_grad, tables)
    filt_re, filt_im = forward_real(own_filter.reshape(own_grp, half_rows, size_two), tables)
    grad_re4 = grad_re.reshape(own_grp, per_group, size_one, size_two)
    grad_im4 = grad_im.reshape(own_grp, per_group, size_one, size_two)
    filt_re4 = filt_re[:, None]
    filt_im4 = filt_im[:, None]
    prod_re = (filt_re4 * grad_re4 + filt_im4 * grad_im4).reshape(own_ch, size_one, size_two)
    prod_im = (filt_re4 * grad_im4 - filt_im4 * grad_re4).reshape(own_ch, size_one, size_two)
    correlated = (
        inverse_real(prod_re, prod_im, tables, half_rows)
        .reshape(1, own_ch, seq_len)
        .astype(jnp.bfloat16)
    )
    returned = lax.all_to_all(correlated, "context", split_axis=2, concat_axis=1, tiled=True)
    grad_input = (
        returned.astype(jnp.float32) + skip[None, :, None] * out_grad.astype(jnp.float32)
    ).astype(jnp.bfloat16)
    in_re4 = in_re.reshape(own_grp, per_group, size_one, size_two)
    in_im4 = in_im.reshape(own_grp, per_group, size_one, size_two)
    lag_re = (in_re4 * grad_re4 + in_im4 * grad_im4).sum(axis=1)
    lag_im = (in_re4 * grad_im4 - in_im4 * grad_re4).sum(axis=1)
    own_terms = inverse_real(lag_re, lag_im, tables, half_rows).reshape(own_grp, seq_len)
    pieces = lax.all_to_all(
        own_terms.reshape(own_grp, owners, tok_dev),
        "context",
        split_axis=1,
        concat_axis=0,
        tiled=True,
    )
    row_groups = owner_groups(owners, own_ch, own_grp).reshape(-1)
    pick_sum = (jnp.arange(grp_dev, dtype=jnp.int32)[:, None] == row_groups[None, :]).astype(
        jnp.float32
    )
    local_sum = jnp.dot(pick_sum, pieces.reshape(owners * own_grp, tok_dev), precision=exact_mode)
    summed = lax.psum(local_sum, "dp")
    norm_scale = 1.0 / math.sqrt(lax.axis_size("dp") * GROUP * seq_len)
    return (grad_input, summed * norm_scale)


def per_device(inputs, out_grad, filters, skip):
    sequences = lax.axis_size("dp")
    halves = lax.axis_size("context") == 2 and inputs.shape[0] == 1
    if halves and sequences & (sequences - 1) == 0 and inputs.shape[1] % (2 * inputs.shape[2]) == 0:
        late = lax.axis_index("tensor") % 2 == 1
        return lax.cond(
            late, functools.partial(paired, True), functools.partial(paired, False), inputs, out_grad, filters, skip
        )
    return owned(inputs, out_grad, filters, skip)


def solution(mesh):
    in_specs = (
        P("dp", "tensor", "context"),
        P("dp", "tensor", "context"),
        P("tensor", "context"),
        P("tensor"),
    )
    out_specs = (P("dp", "tensor", "context"), P("tensor", "context"))
    return jax.shard_map(
        per_device, mesh=mesh, in_specs=in_specs, out_specs=out_specs, check_vma=False
    )
```

```python
import functools
import math

import jax
import jax.numpy as jnp
import numpy as np
from jax import lax
from jax.experimental import pallas as pl
from jax.experimental.pallas import tpu as pltpu
from jax.sharding import PartitionSpec as P

GROUP = 16


exact_mode = lax.Precision.HIGHEST


def block_tables(tok):
    step = np.arange(tok)
    angle = np.pi / tok * np.outer(step, step + 0.5)
    forward = np.concatenate([np.cos(angle), -np.sin(angle)], axis=1)
    inverse = np.concatenate([np.cos(angle).T, -np.sin(angle).T], axis=0) / tok
    pair = []
    for table, axis in ((forward, 0), (inverse, 1)):
        high = table.astype(jnp.bfloat16)
        low = (table - high.astype(np.float64)).astype(jnp.bfloat16)
        pair.append(jnp.asarray(np.concatenate([high, low], axis=axis)))
    return pair


def block_rows(chans):
    return math.gcd(chans // 2, GROUP * 32)


def matmul(left, right):
    return jnp.dot(left, right, preferred_element_type=jnp.float32)


def split(value):
    high = value.astype(jnp.bfloat16)
    return high, (value - high.astype(jnp.float32)).astype(jnp.bfloat16)


def forward_exact(block, forward):
    return matmul(jnp.concatenate([block, block], axis=1), forward)


def forward_float(value, forward):
    high, low = split(value)
    return forward_exact(high, forward) + matmul(low, forward[: value.shape[1]])


def inverse_float(spec, inverse):
    tok = spec.shape[1] // 2
    high, low = split(spec)
    both = matmul(high, inverse)
    return both[:, :tok] + both[:, tok:] + matmul(low, inverse[:, :tok])


def conj_mul(left, right):
    tok = left.shape[1] // 2
    left_re, left_im = left[:, :tok], left[:, tok:]
    right_re, right_im = right[:, :tok], right[:, tok:]
    return (
        left_re * right_re + left_im * right_im,
        left_re * right_im - left_im * right_re,
    )


def group_sum(value):
    rows, width = value.shape
    return value.reshape(rows // GROUP, GROUP, width).sum(axis=1)


def group_spread(value):
    rows, width = value.shape
    return jnp.broadcast_to(value[:, None, :], (rows, GROUP, width)).reshape(rows * GROUP, width)


def sign_row(tok):
    lane = lax.broadcasted_iota(jnp.int32, (1, tok), 1)
    return (1 - 2 * (lane % 2)).astype(jnp.float32)


def local_lag(in_ref, grad_ref, forward_ref, inverse_ref, part_ref, kept_ref, taps_ref, lag_ref):
    first = lax.axis_index("context") == 0
    chans, tok = in_ref.shape
    rows = block_rows(chans)
    forward = forward_ref[...]
    for start in range(0, chans, rows):
        span = pl.ds(start, rows)
        groups = pl.ds(start // GROUP, rows // GROUP)
        in_spec = forward_exact(in_ref[span, :], forward)
        grad_spec = forward_exact(grad_ref[span, :], forward)
        lag_re, lag_im = conj_mul(in_spec, grad_spec)
        lag_ref[groups, :tok] = group_sum(lag_re)
        lag_ref[groups, tok:] = group_sum(lag_im)
        part_ref[span, :] = jnp.where(first, in_spec, grad_spec)
    taps = inverse_float(lag_ref[...], inverse_ref[...])
    kept_ref[...] = jnp.where(first, taps, 0.0)
    taps_ref[...] = jnp.where(first, 0.0, taps)


def local_corr(grad_ref, own_ref, skip_ref, forward_ref, inverse_ref, corr_ref, gained_ref, base_ref):
    first = lax.axis_index("context") == 0
    chans, tok = grad_ref.shape
    rows = block_rows(chans)
    forward = forward_ref[...]
    inverse = inverse_ref[...]
    base_ref[...] = jnp.where(first, forward_float(own_ref[...], forward), 0.0)
    for start in range(0, chans, rows):
        span = pl.ds(start, rows)
        groups = pl.ds(start // GROUP, rows // GROUP)
        grad = grad_ref[span, :]
        spec = forward_exact(grad, forward)
        prod = conj_mul(group_spread(base_ref[groups, :]), spec)
        corr_ref[span, :] = inverse_float(jnp.concatenate(prod, axis=1), inverse)
        for at in range(0, rows, tok):
            gain = jnp.broadcast_to(skip_ref[(start + at) // tok, :][None, :], (tok, tok)).T
            gained_ref[pl.ds(start + at, tok), :] = gain * grad[at : at + tok, :].astype(jnp.float32)


def load_kernel(whole, in_ref, grad_ref, filters_ref, skip_ref, *refs):
    first = lax.axis_index("context") == 0
    *parts, filters_held, skip_held, sems = refs
    pairs = [(filters_ref, filters_held), (skip_ref, skip_held)]
    if whole:
        *parts, in_held, grad_held = parts
        pairs += [(in_ref, in_held), (grad_ref, grad_held)]
    copies = [pltpu.make_async_copy(*pair, sems.at[i]) for i, pair in enumerate(pairs)]

    def fetch(ref):
        copy = pltpu.make_async_copy(ref, parts[0], sems.at[len(copies)])
        copy.start()
        copy.wait()

    for copy in copies:
        copy.start()
    if not whole:
        pl.when(first)(lambda: fetch(in_ref))
        pl.when(jnp.logical_not(first))(lambda: fetch(grad_ref))
    for copy in copies:
        copy.wait()
    if whole:
        start = 0
        for part in parts:
            span = pl.ds(start, part.shape[0])
            part[...] = jnp.where(first, in_held[span, :], grad_held[span, :])
            start += part.shape[0]


def moved_block(parts, start, rows):
    for part in parts:
        if start < part.shape[0]:
            return part[pl.ds(start, rows), :]
        start -= part.shape[0]


def cross_lag_kernel(*refs):
    *parts, part_ref, forward_ref, inverse_ref, out_ref, sum_ref = refs
    first = lax.axis_index("context") == 0
    chans, tok = part_ref.shape[0], out_ref.shape[1]
    rows = block_rows(chans)
    forward = forward_ref[...]
    for start in range(0, chans, rows):
        span = pl.ds(start, rows)
        groups = pl.ds(start // GROUP, rows // GROUP)
        spec = forward_exact(moved_block(parts, start, rows), forward)
        re, im = conj_mul(part_ref[span, :], spec)
        sum_ref[groups, :tok] = group_sum(re)
        sum_ref[groups, tok:] = group_sum(im)
    sign = sign_row(tok)
    re, im = sum_ref[:, :tok], sum_ref[:, tok:]
    total = jnp.concatenate(
        [
            jnp.where(first, sign * im, re),
            -jnp.where(first, sign * re, im),
        ],
        axis=1,
    )
    out_ref[...] = inverse_float(total, inverse_ref[...])


def cross_corr_kernel(*refs):
    *parts, grad_ref, own_ref, other_ref, corr_ref, gained_ref, forward_ref, inverse_ref, out_ref, turn_ref = refs
    first = lax.axis_index("context") == 0
    chans, tok = grad_ref.shape
    rows = block_rows(chans)
    forward = forward_ref[...]
    inverse = inverse_ref[...]
    own = forward_float(own_ref[...], forward)
    other = forward_float(other_ref[...], forward)
    sign = sign_row(tok)
    turn_ref[:, :tok] = other[:, :tok] - jnp.where(first, sign * own[:, tok:], 0.0)
    turn_ref[:, tok:] = other[:, tok:] + jnp.where(first, sign * own[:, :tok], 0.0)
    for start in range(0, chans, rows):
        span = pl.ds(start, rows)
        spec = forward_exact(jnp.where(first, moved_block(parts, start, rows), grad_ref[span, :]), forward)
        turn = group_spread(turn_ref[pl.ds(start // GROUP, rows // GROUP), :])
        corr = corr_ref[span, :] + inverse_float(jnp.concatenate(conj_mul(turn, spec), axis=1), inverse)
        corr = corr.astype(jnp.bfloat16).astype(jnp.float32)
        out_ref[span, :] = (corr + gained_ref[span, :]).astype(jnp.bfloat16)


def finish_kernel(scale, left_ref, right_ref, out_ref):
    out_ref[...] = (left_ref[...] + right_ref[...]) * scale


def store_kernel(held_ref, out_ref, sem):
    copy = pltpu.make_async_copy(held_ref, out_ref, sem)
    copy.start()
    copy.wait()


VMEM_SPEC = pl.BlockSpec(memory_space=pltpu.VMEM)


ANY_SPEC = pl.BlockSpec(memory_space=pl.ANY)


def call(kernel, out_shape, scratch, cost, *operands, in_specs=None, out_specs=None, aliases={}):
    return pl.pallas_call(
        kernel,
        out_shape=out_shape,
        in_specs=in_specs or [VMEM_SPEC] * len(operands),
        input_output_aliases=aliases,
        out_specs=out_specs or jax.tree.map(lambda _: VMEM_SPEC, out_shape),
        scratch_shapes=scratch,
        cost_estimate=pl.CostEstimate(flops=cost, bytes_accessed=cost // 256, transcendentals=0),
        compiler_params=pltpu.CompilerParams(vmem_limit_bytes=24 * 1024 * 1024),
    )(*operands)


def in_vmem(value):
    return pltpu.with_memory_space_constraint(value, pltpu.VMEM)


def paired(late, inputs, out_grad, filters, skip):
    chans, tok = inputs.shape[1:]
    groups = filters.shape[0]
    sequences = lax.axis_size("dp")
    swap = [(0, 1), (1, 0)]
    forward, inverse = block_tables(tok)
    own_in, own_grad = inputs[0], out_grad[0]
    skip_rows = skip.reshape(-1, tok)
    cost = 4 * chans * tok * tok
    wide = pltpu.VMEM((chans, tok), jnp.float32)
    spectra = pltpu.VMEM((groups, 2 * tok), jnp.float32)

    rows = block_rows(chans)
    cut = chans // (2 * rows) * rows
    block = pltpu.VMEM((chans, tok), jnp.bfloat16)
    narrow = pltpu.VMEM((groups, tok), jnp.float32)
    sizes = (cut, chans - cut) if late else (chans,)
    parts = tuple(pltpu.VMEM((size, tok), jnp.bfloat16) for size in sizes)
    loaded = call(
        functools.partial(load_kernel, late),
        parts + ((block, block) if late else ()) + (narrow, pltpu.VMEM(skip_rows.shape, jnp.float32)),
        [pltpu.SemaphoreType.DMA((4,))],
        8 * cost,
        *(pltpu.with_memory_space_constraint(v, pltpu.HBM) for v in (own_in, own_grad, filters, skip_rows)),
        in_specs=[ANY_SPEC] * 4,
    )
    own, skip_held = loaded[-2:]
    if late:
        own_in, own_grad = loaded[2:4]
    moved = [lax.ppermute(loaded[0], "context", swap)]
    part, kept, taps = call(
        local_lag,
        (pltpu.VMEM((chans, 2 * tok), jnp.float32), narrow, narrow),
        [spectra],
        8 * cost,
        own_in, own_grad, forward, inverse,
    )

    def correlate_local(grad):
        return call(local_corr, (wide, wide), [spectra], 8 * cost, grad, own, skip_held, forward, inverse)

    if late:
        corr, gained = correlate_local(own_grad)
        moved[0], rest, taps, part, own = lax.optimization_barrier((moved[0], loaded[1], taps, part, own, corr))[:5]
        moved.append(lax.ppermute(rest, "context", swap))
        taps, own = lax.optimization_barrier((taps, own))
    other_taps = lax.ppermute(taps, "context", swap)
    if not late:
        corr, gained = correlate_local(own_grad)
        own, part, corr = lax.optimization_barrier((own, part, corr))
    other_filters = lax.ppermute(own, "context", swap)
    total = (kept + other_taps) + call(
        cross_lag_kernel,
        narrow,
        [spectra],
        8 * cost,
        *map(in_vmem, moved), part, forward, inverse,
    )

    def correlate(filters):
        return call(
            cross_corr_kernel,
            pltpu.VMEM((chans, tok), jnp.bfloat16),
            [spectra],
            8 * cost,
            *map(in_vmem, moved), own_grad, own, in_vmem(filters), corr, gained, forward, inverse,
        )

    norm_scale = 1.0 / math.sqrt(sequences * GROUP * 2 * tok)
    got, step = jnp.zeros_like(total), 1
    grad_input = correlate(other_filters) if late else None
    while step < sequences:
        got = lax.ppermute(total, "dp", [(i, i ^ step) for i in range(sequences)])
        step *= 2
        if step < sequences:
            if late:
                got, grad_input = lax.optimization_barrier((got, grad_input))
            else:
                got, corr = lax.optimization_barrier((got, corr))
            total = total + got
    if not late:
        grad_input = correlate(other_filters)
    stored = call(
        store_kernel,
        jax.ShapeDtypeStruct((chans, tok), jnp.bfloat16),
        [pltpu.SemaphoreType.DMA],
        cost,
        in_vmem(grad_input),
        out_specs=ANY_SPEC,
    )
    got, _ = lax.optimization_barrier((got, stored))
    grad_filter = call(
        functools.partial(finish_kernel, norm_scale),
        jax.ShapeDtypeStruct((groups, tok), jnp.float32),
        [],
        cost,
        total, got,
    )
    return (stored[None], grad_filter)


def dft_tables(size_one, size_two):
    padded_len = size_one * size_two
    range_one = jnp.arange(size_one, dtype=jnp.int32)
    range_two = jnp.arange(size_two, dtype=jnp.int32)
    angle_one = (range_one[:, None] * range_one[None, :] % size_one).astype(jnp.float32) * (
        -2.0 * math.pi / size_one
    )
    angle_two = (range_two[:, None] * range_two[None, :] % size_two).astype(jnp.float32) * (
        -2.0 * math.pi / size_two
    )
    angle_turn = (range_one[:, None] * range_two[None, :] % padded_len).astype(jnp.float32) * (
        -2.0 * math.pi / padded_len
    )
    return (
        jnp.cos(angle_one),
        jnp.sin(angle_one),
        jnp.cos(angle_two),
        jnp.sin(angle_two),
        jnp.cos(angle_turn),
        jnp.sin(angle_turn),
    )


def left_mul(matrix, operand):
    return jnp.einsum("kj,mjl->mkl", matrix, operand, precision=exact_mode)


def right_mul(operand, matrix):
    return jnp.einsum("mkj,jl->mkl", operand, matrix, precision=exact_mode)


def forward_real(signal, tables):
    one_re, one_im, two_re, two_im, turn_re, turn_im = tables
    half_rows = signal.shape[1]
    step_re = left_mul(one_re[:, :half_rows], signal)
    step_im = left_mul(one_im[:, :half_rows], signal)
    mid_re = step_re * turn_re - step_im * turn_im
    mid_im = step_re * turn_im + step_im * turn_re
    spec_re = right_mul(mid_re, two_re) - right_mul(mid_im, two_im)
    spec_im = right_mul(mid_re, two_im) + right_mul(mid_im, two_re)
    return (spec_re, spec_im)


def inverse_real(spec_re, spec_im, tables, half_rows):
    one_re, one_im, two_re, two_im, turn_re, turn_im = tables
    back_re = right_mul(spec_re, two_re) + right_mul(spec_im, two_im)
    back_im = right_mul(spec_im, two_re) - right_mul(spec_re, two_im)
    mid_re = back_re * turn_re + back_im * turn_im
    mid_im = back_im * turn_re - back_re * turn_im
    padded_len = one_re.shape[0] * two_re.shape[0]
    return (
        left_mul(one_re[:half_rows], mid_re) + left_mul(one_im[:half_rows], mid_im)
    ) / padded_len


def owner_groups(owners, own_ch, own_grp):
    starts = jnp.arange(owners, dtype=jnp.int32)[:, None] * own_ch // GROUP
    return starts + jnp.arange(own_grp, dtype=jnp.int32)[None, :]


def owned(inputs, out_grad, filters, skip):
    tok_dev = inputs.shape[2]
    ch_dev = inputs.shape[1]
    grp_dev = filters.shape[0]
    owners = lax.axis_size("context")
    seq_len = tok_dev * owners
    padded_len = 2 * seq_len
    own_ch = ch_dev // owners
    own_grp = max(1, own_ch // GROUP)
    per_group = own_ch // own_grp
    size_one = 1 << (padded_len.bit_length() - 1) // 2
    while padded_len % size_one != 0:
        size_one = size_one // 2
    size_two = padded_len // size_one
    half_rows = size_one // 2
    tables = dft_tables(size_one, size_two)
    moved_in, moved_grad = (
        lax.all_to_all(inputs, "context", split_axis=1, concat_axis=2, tiled=True),
        lax.all_to_all(out_grad, "context", split_axis=1, concat_axis=2, tiled=True),
    )
    slot_groups = owner_groups(owners, own_ch, own_grp)
    pick_rows = (
        slot_groups[:, :, None] == jnp.arange(grp_dev, dtype=jnp.int32)[None, None, :]
    ).astype(jnp.float32)
    outgoing = jnp.einsum("ojg,gt->ojt", pick_rows, filters, precision=exact_mode)
    own_filter = lax.all_to_all(
        outgoing, "context", split_axis=0, concat_axis=2, tiled=True
    ).reshape(own_grp, seq_len)
    sig_in = moved_in[0].astype(jnp.float32).reshape(own_ch, half_rows, size_two)
    sig_grad = moved_grad[0].astype(jnp.float32).reshape(own_ch, half_rows, size_two)
    in_re, in_im = forward_real(sig_in, tables)
    grad_re, grad_im = forward_real(sig_grad, tables)
    filt_re, filt_im = forward_real(own_filter.reshape(own_grp, half_rows, size_two), tables)
    grad_re4 = grad_re.reshape(own_grp, per_group, size_one, size_two)
    grad_im4 = grad_im.reshape(own_grp, per_group, size_one, size_two)
    filt_re4 = filt_re[:, None]
    filt_im4 = filt_im[:, None]
    prod_re = (filt_re4 * grad_re4 + filt_im4 * grad_im4).reshape(own_ch, size_one, size_two)
    prod_im = (filt_re4 * grad_im4 - filt_im4 * grad_re4).reshape(own_ch, size_one, size_two)
    correlated = (
        inverse_real(prod_re, prod_im, tables, half_rows)
        .reshape(1, own_ch, seq_len)
        .astype(jnp.bfloat16)
    )
    returned = lax.all_to_all(correlated, "context", split_axis=2, concat_axis=1, tiled=True)
    grad_input = (
        returned.astype(jnp.float32) + skip[None, :, None] * out_grad.astype(jnp.float32)
    ).astype(jnp.bfloat16)
    in_re4 = in_re.reshape(own_grp, per_group, size_one, size_two)
    in_im4 = in_im.reshape(own_grp, per_group, size_one, size_two)
    lag_re = (in_re4 * grad_re4 + in_im4 * grad_im4).sum(axis=1)
    lag_im = (in_re4 * grad_im4 - in_im4 * grad_re4).sum(axis=1)
    own_terms = inverse_real(lag_re, lag_im, tables, half_rows).reshape(own_grp, seq_len)
    pieces = lax.all_to_all(
        own_terms.reshape(own_grp, owners, tok_dev),
        "context",
        split_axis=1,
        concat_axis=0,
        tiled=True,
    )
    row_groups = owner_groups(owners, own_ch, own_grp).reshape(-1)
    pick_sum = (jnp.arange(grp_dev, dtype=jnp.int32)[:, None] == row_groups[None, :]).astype(
        jnp.float32
    )
    local_sum = jnp.dot(pick_sum, pieces.reshape(owners * own_grp, tok_dev), precision=exact_mode)
    summed = lax.psum(local_sum, "dp")
    norm_scale = 1.0 / math.sqrt(lax.axis_size("dp") * GROUP * seq_len)
    return (grad_input, summed * norm_scale)


def per_device(inputs, out_grad, filters, skip):
    sequences = lax.axis_size("dp")
    halves = lax.axis_size("context") == 2 and inputs.shape[0] == 1
    if halves and sequences & (sequences - 1) == 0 and inputs.shape[1] % (2 * inputs.shape[2]) == 0:
        late = lax.axis_index("tensor") % 2 == 1
        return lax.cond(
            late, functools.partial(paired, True), functools.partial(paired, False), inputs, out_grad, filters, skip
        )
    return owned(inputs, out_grad, filters, skip)


def solution(mesh):
    in_specs = (
        P("dp", "tensor", "context"),
        P("dp", "tensor", "context"),
        P("tensor", "context"),
        P("tensor"),
    )
    out_specs = (P("dp", "tensor", "context"), P("tensor", "context"))
    return jax.shard_map(
        per_device, mesh=mesh, in_specs=in_specs, out_specs=out_specs, check_vma=False
    )
```

```python
import functools
import math

import jax
import jax.numpy as jnp
import numpy as np
from jax import lax
from jax.experimental import pallas as pl
from jax.experimental.pallas import tpu as pltpu
from jax.sharding import PartitionSpec as P

GROUP = 16


exact_mode = lax.Precision.HIGHEST


def block_tables(tok):
    step = np.arange(tok)
    angle = np.pi / tok * np.outer(step, step + 0.5)
    forward = np.concatenate([np.cos(angle), -np.sin(angle)], axis=1)
    inverse = np.concatenate([np.cos(angle).T, -np.sin(angle).T], axis=0) / tok
    pair = []
    for table, axis in ((forward, 0), (inverse, 1)):
        high = table.astype(jnp.bfloat16)
        low = (table - high.astype(np.float64)).astype(jnp.bfloat16)
        pair.append(jnp.asarray(np.concatenate([high, low], axis=axis)))
    return pair


def block_rows(chans):
    return math.gcd(chans // 2, GROUP * 32)


def matmul(left, right):
    return jnp.dot(left, right, preferred_element_type=jnp.float32)


def split(value):
    high = value.astype(jnp.bfloat16)
    return high, (value - high.astype(jnp.float32)).astype(jnp.bfloat16)


def forward_exact(block, forward):
    return matmul(jnp.concatenate([block, block], axis=1), forward)


def forward_float(value, forward):
    high, low = split(value)
    return forward_exact(high, forward) + matmul(low, forward[: value.shape[1]])


def inverse_float(spec, inverse):
    tok = spec.shape[1] // 2
    high, low = split(spec)
    both = matmul(high, inverse)
    return both[:, :tok] + both[:, tok:] + matmul(low, inverse[:, :tok])


def conj_mul(left, right):
    tok = left.shape[1] // 2
    left_re, left_im = left[:, :tok], left[:, tok:]
    right_re, right_im = right[:, :tok], right[:, tok:]
    return (
        left_re * right_re + left_im * right_im,
        left_re * right_im - left_im * right_re,
    )


def group_sum(value):
    rows, width = value.shape
    return value.reshape(rows // GROUP, GROUP, width).sum(axis=1)


def group_spread(value):
    rows, width = value.shape
    return jnp.broadcast_to(value[:, None, :], (rows, GROUP, width)).reshape(rows * GROUP, width)


def sign_row(tok):
    lane = lax.broadcasted_iota(jnp.int32, (1, tok), 1)
    return (1 - 2 * (lane % 2)).astype(jnp.float32)


def local_lag(in_ref, grad_ref, forward_ref, inverse_ref, part_ref, kept_ref, taps_ref, lag_ref):
    first = lax.axis_index("context") == 0
    chans, tok = in_ref.shape
    rows = block_rows(chans)
    forward = forward_ref[...]
    for start in range(0, chans, rows):
        span = pl.ds(start, rows)
        groups = pl.ds(start // GROUP, rows // GROUP)
        in_spec = forward_exact(in_ref[span, :], forward)
        grad_spec = forward_exact(grad_ref[span, :], forward)
        lag_re, lag_im = conj_mul(in_spec, grad_spec)
        lag_ref[groups, :tok] = group_sum(lag_re)
        lag_ref[groups, tok:] = group_sum(lag_im)
        part_ref[span, :] = jnp.where(first, in_spec, grad_spec)
    taps = inverse_float(lag_ref[...], inverse_ref[...])
    kept_ref[...] = jnp.where(first, taps, 0.0)
    taps_ref[...] = jnp.where(first, 0.0, taps)


def local_corr(grad_ref, own_ref, skip_ref, forward_ref, inverse_ref, corr_ref, gained_ref, base_ref):
    first = lax.axis_index("context") == 0
    chans, tok = grad_ref.shape
    rows = block_rows(chans)
    forward = forward_ref[...]
    inverse = inverse_ref[...]
    base_ref[...] = jnp.where(first, forward_float(own_ref[...], forward), 0.0)
    for start in range(0, chans, rows):
        span = pl.ds(start, rows)
        groups = pl.ds(start // GROUP, rows // GROUP)
        grad = grad_ref[span, :]
        spec = forward_exact(grad, forward)
        prod = conj_mul(group_spread(base_ref[groups, :]), spec)
        corr_ref[span, :] = inverse_float(jnp.concatenate(prod, axis=1), inverse)
        for at in range(0, rows, tok):
            gain = jnp.broadcast_to(skip_ref[(start + at) // tok, :][None, :], (tok, tok)).T
            gained_ref[pl.ds(start + at, tok), :] = gain * grad[at : at + tok, :].astype(jnp.float32)


def load_kernel(in_ref, grad_ref, filters_ref, skip_ref, *refs):
    first = lax.axis_index("context") == 0
    *parts, in_held, grad_held, filters_held, skip_held, sems = refs
    pairs = ((in_ref, in_held), (grad_ref, grad_held), (filters_ref, filters_held), (skip_ref, skip_held))
    copies = [pltpu.make_async_copy(*pair, sems.at[i]) for i, pair in enumerate(pairs)]
    for copy in copies:
        copy.start()
    for copy in copies:
        copy.wait()
    start = 0
    for part in parts:
        span = pl.ds(start, part.shape[0])
        part[...] = jnp.where(first, in_held[span, :], grad_held[span, :])
        start += part.shape[0]


def moved_block(parts, start, rows):
    for part in parts:
        if start < part.shape[0]:
            return part[pl.ds(start, rows), :]
        start -= part.shape[0]


def cross_lag_kernel(*refs):
    *parts, part_ref, forward_ref, inverse_ref, out_ref, sum_ref = refs
    first = lax.axis_index("context") == 0
    chans, tok = part_ref.shape[0], out_ref.shape[1]
    rows = block_rows(chans)
    forward = forward_ref[...]
    for start in range(0, chans, rows):
        span = pl.ds(start, rows)
        groups = pl.ds(start // GROUP, rows // GROUP)
        spec = forward_exact(moved_block(parts, start, rows), forward)
        re, im = conj_mul(part_ref[span, :], spec)
        sum_ref[groups, :tok] = group_sum(re)
        sum_ref[groups, tok:] = group_sum(im)
    sign = sign_row(tok)
    re, im = sum_ref[:, :tok], sum_ref[:, tok:]
    total = jnp.concatenate(
        [
            jnp.where(first, sign * im, re),
            -jnp.where(first, sign * re, im),
        ],
        axis=1,
    )
    out_ref[...] = inverse_float(total, inverse_ref[...])


def cross_corr_kernel(*refs):
    *parts, grad_ref, own_ref, other_ref, corr_ref, gained_ref, forward_ref, inverse_ref, out_ref, turn_ref = refs
    first = lax.axis_index("context") == 0
    chans, tok = grad_ref.shape
    rows = block_rows(chans)
    forward = forward_ref[...]
    inverse = inverse_ref[...]
    own = forward_float(own_ref[...], forward)
    other = forward_float(other_ref[...], forward)
    sign = sign_row(tok)
    turn_ref[:, :tok] = other[:, :tok] - jnp.where(first, sign * own[:, tok:], 0.0)
    turn_ref[:, tok:] = other[:, tok:] + jnp.where(first, sign * own[:, :tok], 0.0)
    for start in range(0, chans, rows):
        span = pl.ds(start, rows)
        spec = forward_exact(jnp.where(first, moved_block(parts, start, rows), grad_ref[span, :]), forward)
        turn = group_spread(turn_ref[pl.ds(start // GROUP, rows // GROUP), :])
        corr = corr_ref[span, :] + inverse_float(jnp.concatenate(conj_mul(turn, spec), axis=1), inverse)
        corr = corr.astype(jnp.bfloat16).astype(jnp.float32)
        out_ref[span, :] = (corr + gained_ref[span, :]).astype(jnp.bfloat16)


def finish_kernel(scale, left_ref, right_ref, out_ref):
    out_ref[...] = (left_ref[...] + right_ref[...]) * scale


def store_kernel(held_ref, out_ref, sem):
    copy = pltpu.make_async_copy(held_ref, out_ref, sem)
    copy.start()
    copy.wait()


VMEM_SPEC = pl.BlockSpec(memory_space=pltpu.VMEM)


ANY_SPEC = pl.BlockSpec(memory_space=pl.ANY)


def call(kernel, out_shape, scratch, cost, *operands, in_specs=None, out_specs=None, aliases={}):
    return pl.pallas_call(
        kernel,
        out_shape=out_shape,
        in_specs=in_specs or [VMEM_SPEC] * len(operands),
        input_output_aliases=aliases,
        out_specs=out_specs or jax.tree.map(lambda _: VMEM_SPEC, out_shape),
        scratch_shapes=scratch,
        cost_estimate=pl.CostEstimate(flops=cost, bytes_accessed=cost // 256, transcendentals=0),
        compiler_params=pltpu.CompilerParams(vmem_limit_bytes=24 * 1024 * 1024),
    )(*operands)


def in_vmem(value):
    return pltpu.with_memory_space_constraint(value, pltpu.VMEM)


def paired(late, inputs, out_grad, filters, skip):
    chans, tok = inputs.shape[1:]
    groups = filters.shape[0]
    sequences = lax.axis_size("dp")
    swap = [(0, 1), (1, 0)]
    forward, inverse = block_tables(tok)
    own_in, own_grad = inputs[0], out_grad[0]
    skip_rows = skip.reshape(-1, tok)
    cost = 4 * chans * tok * tok
    wide = pltpu.VMEM((chans, tok), jnp.float32)
    spectra = pltpu.VMEM((groups, 2 * tok), jnp.float32)

    rows = block_rows(chans)
    cut = chans // (2 * rows) * rows
    block = pltpu.VMEM((chans, tok), jnp.bfloat16)
    narrow = pltpu.VMEM((groups, tok), jnp.float32)
    sizes = (cut, chans - cut) if late else (chans,)
    parts = tuple(pltpu.VMEM((size, tok), jnp.bfloat16) for size in sizes)
    loaded = call(
        load_kernel,
        parts + (block, block, narrow, pltpu.VMEM(skip_rows.shape, jnp.float32)),
        [pltpu.SemaphoreType.DMA((4,))],
        cost,
        *(pltpu.with_memory_space_constraint(v, pltpu.HBM) for v in (own_in, own_grad, filters, skip_rows)),
        in_specs=[ANY_SPEC] * 4,
    )
    own_in, own_grad, own, skip_held = loaded[-4:]
    moved = [lax.ppermute(loaded[0], "context", swap)]
    part, kept, taps = call(
        local_lag,
        (pltpu.VMEM((chans, 2 * tok), jnp.float32), narrow, narrow),
        [spectra],
        8 * cost,
        own_in, own_grad, forward, inverse,
    )

    def correlate_local(grad):
        return call(local_corr, (wide, wide), [spectra], 8 * cost, grad, own, skip_held, forward, inverse)

    if late:
        corr, gained = correlate_local(own_grad)
        moved[0], rest, taps, part, own = lax.optimization_barrier((moved[0], loaded[1], taps, part, own, corr))[:5]
        moved.append(lax.ppermute(rest, "context", swap))
        taps, own = lax.optimization_barrier((taps, own))
    if not late:
        corr, gained = correlate_local(own_grad)
        own, part, corr, taps = lax.optimization_barrier((own, part, corr, taps))
    other_taps = lax.ppermute(taps, "context", swap)
    other_filters = lax.ppermute(own, "context", swap)
    total = (kept + other_taps) + call(
        cross_lag_kernel,
        narrow,
        [spectra],
        8 * cost,
        *map(in_vmem, moved), part, forward, inverse,
    )

    def correlate(filters):
        return call(
            cross_corr_kernel,
            pltpu.VMEM((chans, tok), jnp.bfloat16),
            [spectra],
            8 * cost,
            *map(in_vmem, moved), own_grad, own, in_vmem(filters), corr, gained, forward, inverse,
        )

    norm_scale = 1.0 / math.sqrt(sequences * GROUP * 2 * tok)
    got, step = jnp.zeros_like(total), 1
    grad_input = correlate(other_filters) if late else None
    while step < sequences:
        got = lax.ppermute(total, "dp", [(i, i ^ step) for i in range(sequences)])
        step *= 2
        if step < sequences:
            if late:
                got, grad_input = lax.optimization_barrier((got, grad_input))
            else:
                got, corr = lax.optimization_barrier((got, corr))
            total = total + got
    if not late:
        grad_input = correlate(other_filters)
    stored = call(
        store_kernel,
        jax.ShapeDtypeStruct((chans, tok), jnp.bfloat16),
        [pltpu.SemaphoreType.DMA],
        cost,
        in_vmem(grad_input),
        out_specs=ANY_SPEC,
    )
    got, _ = lax.optimization_barrier((got, stored))
    grad_filter = call(
        functools.partial(finish_kernel, norm_scale),
        jax.ShapeDtypeStruct((groups, tok), jnp.float32),
        [],
        cost,
        total, got,
    )
    return (stored[None], grad_filter)


def dft_tables(size_one, size_two):
    padded_len = size_one * size_two
    range_one = jnp.arange(size_one, dtype=jnp.int32)
    range_two = jnp.arange(size_two, dtype=jnp.int32)
    angle_one = (range_one[:, None] * range_one[None, :] % size_one).astype(jnp.float32) * (
        -2.0 * math.pi / size_one
    )
    angle_two = (range_two[:, None] * range_two[None, :] % size_two).astype(jnp.float32) * (
        -2.0 * math.pi / size_two
    )
    angle_turn = (range_one[:, None] * range_two[None, :] % padded_len).astype(jnp.float32) * (
        -2.0 * math.pi / padded_len
    )
    return (
        jnp.cos(angle_one),
        jnp.sin(angle_one),
        jnp.cos(angle_two),
        jnp.sin(angle_two),
        jnp.cos(angle_turn),
        jnp.sin(angle_turn),
    )


def left_mul(matrix, operand):
    return jnp.einsum("kj,mjl->mkl", matrix, operand, precision=exact_mode)


def right_mul(operand, matrix):
    return jnp.einsum("mkj,jl->mkl", operand, matrix, precision=exact_mode)


def forward_real(signal, tables):
    one_re, one_im, two_re, two_im, turn_re, turn_im = tables
    half_rows = signal.shape[1]
    step_re = left_mul(one_re[:, :half_rows], signal)
    step_im = left_mul(one_im[:, :half_rows], signal)
    mid_re = step_re * turn_re - step_im * turn_im
    mid_im = step_re * turn_im + step_im * turn_re
    spec_re = right_mul(mid_re, two_re) - right_mul(mid_im, two_im)
    spec_im = right_mul(mid_re, two_im) + right_mul(mid_im, two_re)
    return (spec_re, spec_im)


def inverse_real(spec_re, spec_im, tables, half_rows):
    one_re, one_im, two_re, two_im, turn_re, turn_im = tables
    back_re = right_mul(spec_re, two_re) + right_mul(spec_im, two_im)
    back_im = right_mul(spec_im, two_re) - right_mul(spec_re, two_im)
    mid_re = back_re * turn_re + back_im * turn_im
    mid_im = back_im * turn_re - back_re * turn_im
    padded_len = one_re.shape[0] * two_re.shape[0]
    return (
        left_mul(one_re[:half_rows], mid_re) + left_mul(one_im[:half_rows], mid_im)
    ) / padded_len


def owner_groups(owners, own_ch, own_grp):
    starts = jnp.arange(owners, dtype=jnp.int32)[:, None] * own_ch // GROUP
    return starts + jnp.arange(own_grp, dtype=jnp.int32)[None, :]


def owned(inputs, out_grad, filters, skip):
    tok_dev = inputs.shape[2]
    ch_dev = inputs.shape[1]
    grp_dev = filters.shape[0]
    owners = lax.axis_size("context")
    seq_len = tok_dev * owners
    padded_len = 2 * seq_len
    own_ch = ch_dev // owners
    own_grp = max(1, own_ch // GROUP)
    per_group = own_ch // own_grp
    size_one = 1 << (padded_len.bit_length() - 1) // 2
    while padded_len % size_one != 0:
        size_one = size_one // 2
    size_two = padded_len // size_one
    half_rows = size_one // 2
    tables = dft_tables(size_one, size_two)
    moved_in, moved_grad = (
        lax.all_to_all(inputs, "context", split_axis=1, concat_axis=2, tiled=True),
        lax.all_to_all(out_grad, "context", split_axis=1, concat_axis=2, tiled=True),
    )
    slot_groups = owner_groups(owners, own_ch, own_grp)
    pick_rows = (
        slot_groups[:, :, None] == jnp.arange(grp_dev, dtype=jnp.int32)[None, None, :]
    ).astype(jnp.float32)
    outgoing = jnp.einsum("ojg,gt->ojt", pick_rows, filters, precision=exact_mode)
    own_filter = lax.all_to_all(
        outgoing, "context", split_axis=0, concat_axis=2, tiled=True
    ).reshape(own_grp, seq_len)
    sig_in = moved_in[0].astype(jnp.float32).reshape(own_ch, half_rows, size_two)
    sig_grad = moved_grad[0].astype(jnp.float32).reshape(own_ch, half_rows, size_two)
    in_re, in_im = forward_real(sig_in, tables)
    grad_re, grad_im = forward_real(sig_grad, tables)
    filt_re, filt_im = forward_real(own_filter.reshape(own_grp, half_rows, size_two), tables)
    grad_re4 = grad_re.reshape(own_grp, per_group, size_one, size_two)
    grad_im4 = grad_im.reshape(own_grp, per_group, size_one, size_two)
    filt_re4 = filt_re[:, None]
    filt_im4 = filt_im[:, None]
    prod_re = (filt_re4 * grad_re4 + filt_im4 * grad_im4).reshape(own_ch, size_one, size_two)
    prod_im = (filt_re4 * grad_im4 - filt_im4 * grad_re4).reshape(own_ch, size_one, size_two)
    correlated = (
        inverse_real(prod_re, prod_im, tables, half_rows)
        .reshape(1, own_ch, seq_len)
        .astype(jnp.bfloat16)
    )
    returned = lax.all_to_all(correlated, "context", split_axis=2, concat_axis=1, tiled=True)
    grad_input = (
        returned.astype(jnp.float32) + skip[None, :, None] * out_grad.astype(jnp.float32)
    ).astype(jnp.bfloat16)
    in_re4 = in_re.reshape(own_grp, per_group, size_one, size_two)
    in_im4 = in_im.reshape(own_grp, per_group, size_one, size_two)
    lag_re = (in_re4 * grad_re4 + in_im4 * grad_im4).sum(axis=1)
    lag_im = (in_re4 * grad_im4 - in_im4 * grad_re4).sum(axis=1)
    own_terms = inverse_real(lag_re, lag_im, tables, half_rows).reshape(own_grp, seq_len)
    pieces = lax.all_to_all(
        own_terms.reshape(own_grp, owners, tok_dev),
        "context",
        split_axis=1,
        concat_axis=0,
        tiled=True,
    )
    row_groups = owner_groups(owners, own_ch, own_grp).reshape(-1)
    pick_sum = (jnp.arange(grp_dev, dtype=jnp.int32)[:, None] == row_groups[None, :]).astype(
        jnp.float32
    )
    local_sum = jnp.dot(pick_sum, pieces.reshape(owners * own_grp, tok_dev), precision=exact_mode)
    summed = lax.psum(local_sum, "dp")
    norm_scale = 1.0 / math.sqrt(lax.axis_size("dp") * GROUP * seq_len)
    return (grad_input, summed * norm_scale)


def per_device(inputs, out_grad, filters, skip):
    sequences = lax.axis_size("dp")
    halves = lax.axis_size("context") == 2 and inputs.shape[0] == 1
    if halves and sequences & (sequences - 1) == 0 and inputs.shape[1] % (2 * inputs.shape[2]) == 0:
        late = lax.axis_index("tensor") % 2 == 1
        return lax.cond(
            late, functools.partial(paired, True), functools.partial(paired, False), inputs, out_grad, filters, skip
        )
    return owned(inputs, out_grad, filters, skip)


def solution(mesh):
    in_specs = (
        P("dp", "tensor", "context"),
        P("dp", "tensor", "context"),
        P("tensor", "context"),
        P("tensor"),
    )
    out_specs = (P("dp", "tensor", "context"), P("tensor", "context"))
    return jax.shard_map(
        per_device, mesh=mesh, in_specs=in_specs, out_specs=out_specs, check_vma=False
    )
```
